256 devices in a mesh: tm: 32 (over z, y), rows: 8 (over x, core).
Axes of the slice: x: 4, y: 4, z: 8, core: 2. Of those that a mesh axis runs over, the one named last changes fastest.
Arguments:
- source: bfloat16 [128, 8, 32, 256], P('tm', 'rows'), may hold values from -6 to 6
- frame_counts: int32 [32], P('tm'), may hold values from 1 to 9, as said below
- tap_frames: int32 [288, 4], P('tm'), may hold values from 0 to 127, as said below
- tap_weights: float32 [288, 4], P('tm'), may hold values from 0.1 to 0.6
- kernel_one: bfloat16 [3, 3, 3, 256, 256], replicated, may hold values from -0.078125 to 0.078125
- bias_one: float32 [256], replicated, may hold values from -3 to 3
- kernel_two: bfloat16 [3, 3, 3, 256, 256], replicated, may hold values from -0.078125 to 0.078125
- bias_two: float32 [256], replicated, may hold values from -3 to 3
- upstream: bfloat16 [288, 8, 32, 256], P('tm', 'rows'), may hold values from -6 to 6
Outputs:
- decoded: bfloat16 [288, 8, 32, 256], P('tm', 'rows')
- source_grad: float32 [128, 8, 32, 256], P('tm', 'rows')
The draws below stay inside these ranges and needn't reach their ends.
Inputs may be any that keep to these rules, and one draw needn't show every extreme that they name: `frame_counts`: counts of spans 2i and 2i + 1 sum to 10; some span holds exactly 9 frames. `tap_frames`: every tap of a used slot of span d lies in source frames 4 * d - 6 to 4 * d + 9; some span reaches the lower end and some span the upper end. Taps of unused slots are ignored.
All inputs are finite; a program needn't handle non-finite values.
Results may differ from the reference program's by a relative error of at most 0.014.
Values may be sent and summed in bfloat16 or wider, within the bound.
A program may use at most 64 MiB of HBM per device.

```python
import jax
import jax.numpy as jnp
from jax import lax

C = 256
W = 32
FIN_DEV = 4
FOUT_DEV = 5
TAPS = 4
CAP = 9
T_IN = 128
T_OUT = 160
SLOTS = 288
H = 8


def frame_plan(key):
    spans = SLOTS // CAP
    pairs = spans // 2
    key_shift, key_pick, key_jitter = jax.random.split(key, 3)
    moved = jax.random.randint(key_shift, (pairs,), -(FOUT_DEV - 1), FOUT_DEV)
    chosen = jax.random.randint(key_pick, (), 0, pairs - 1)
    pair_ids = jnp.arange(pairs)
    moved = jnp.where(pair_ids == chosen, FOUT_DEV - 1, moved)
    moved = jnp.where(pair_ids == chosen + 1, -(FOUT_DEV - 1), moved)
    counts = jnp.stack([FOUT_DEV + moved, FOUT_DEV - moved], 1).reshape(spans).astype(jnp.int32)
    starts = jnp.cumsum(counts) - counts
    slot_pos = jnp.arange(CAP)
    frames = starts[:, None] + jnp.minimum(slot_pos[None, :], counts[:, None] - 1)
    centre = frames * FIN_DEV // FOUT_DEV
    jitter = jax.random.randint(key_jitter, (spans, CAP), -1, 2)
    span_ids = jnp.arange(spans)
    jitter = jnp.where((span_ids[:, None] == 2 * chosen) & (slot_pos[None, :] == CAP - 1), 1, jitter)
    jitter = jnp.where((span_ids[:, None] == 2 * chosen + 3) & (slot_pos[None, :] == 0), -1, jitter)
    taps = centre[:, :, None] + jitter[:, :, None] - 1 + jnp.arange(TAPS)[None, None, :]
    taps = jnp.clip(taps, 0, spans * FIN_DEV - 1)
    return (counts, taps.reshape(SLOTS, TAPS).astype(jnp.int32))


def draw_frame_counts(key, part):
    counts, taps = frame_plan(key)
    return counts


def draw_tap_frames(key, part):
    counts, taps = frame_plan(key)
    return taps


def steps_of(stream_key, shape, shards, smallest, largest):
    def one(position, shards_of):
        steps = jax.random.uniform(jax.random.fold_in(jax.random.fold_in(stream_key, 6), position), (shards_of,), jnp.float32, smallest / len(shards), largest / len(shards))
        return jnp.repeat(jnp.exp(steps), shape[position] // shards_of).reshape((-1,) + (1,) * (len(shape) - position - 1))

    factor_of = one(*shards[0])
    for cut in shards[1:]:
        factor_of = factor_of * one(*cut)
    return factor_of


def normal_values(rng, dims, width, reach, cuts=(), kind=jnp.bfloat16):
    entries = width * jax.random.normal(rng, dims, jnp.float32)
    if cuts:
        entries = entries * steps_of(rng, dims, cuts, -0.22, 0.18)
    return jnp.clip(entries, -reach, reach).astype(kind)


def setup_inputs(seed: int = 0) -> dict:
    splits = jax.random.split(jax.random.key(seed), 10)
    return {
        "source": normal_values(splits[0], (T_IN, H, W, C), 1.0, 6.0, ((0, 32), (1, 8))),
        "frame_counts": draw_frame_counts(jax.random.fold_in(splits[9], 71), 0),
        "tap_frames": draw_tap_frames(jax.random.fold_in(splits[9], 71), 0),
        "tap_weights": jnp.clip(0.1 + 0.5 * jax.random.uniform(splits[3], (SLOTS, TAPS), jnp.float32) ** steps_of(splits[3], (SLOTS, TAPS), ((0, 32),), -0.2, 0.2), 0.1, 0.6),
        "kernel_one": normal_values(splits[4], (3, 3, 3, C, C), (27 * C) ** -0.5, 0.078125),
        "bias_one": normal_values(splits[5], (C,), 0.5, 3.0, (), jnp.float32),
        "kernel_two": normal_values(splits[6], (3, 3, 3, C, C), (27 * C) ** -0.5, 0.078125),
        "bias_two": normal_values(splits[7], (C,), 0.5, 3.0, (), jnp.float32),
        "upstream": normal_values(splits[8], (SLOTS, H, W, C), 1.0, 6.0, ((0, 32), (1, 8))),
    }


def convolve(field, kernel):
    return lax.conv_general_dilated(field[None], kernel, (1, 1, 1), ((1, 1), (1, 1), (1, 1)), dimension_numbers=("NDHWC", "DHWIO", "NDHWC"), preferred_element_type=jnp.float32)[0]


def forward_block(inputs, kernel, bias):
    widened = inputs.astype(jnp.float32)
    activated = jax.nn.silu(widened).astype(jnp.bfloat16)
    return (widened + convolve(activated, kernel) + bias).astype(jnp.bfloat16)


def backward_block(gradient, inputs, kernel):
    widened = inputs.astype(jnp.float32)
    logistic = jax.nn.sigmoid(widened)
    deriv = logistic * (1.0 + widened * (1.0 - logistic))
    flipped = jnp.transpose(jnp.flip(kernel, (0, 1, 2)), (0, 1, 2, 4, 3))
    return gradient.astype(jnp.float32) + deriv * convolve(gradient, flipped)


def reference(source, frame_counts, tap_frames, tap_weights, kernel_one, bias_one, kernel_two, bias_two, upstream):
    counts = frame_counts.astype(jnp.int32)
    starts = (jnp.cumsum(counts) - counts).astype(jnp.int32)
    slot_pos = jnp.arange(CAP, dtype=jnp.int32)
    in_use = slot_pos[None, :] < counts[:, None]
    frame_of = jnp.where(in_use, starts[:, None] + slot_pos[None, :], T_OUT).reshape(-1).astype(jnp.int32)
    slot_of = jnp.zeros((T_OUT,), jnp.int32).at[frame_of].set(jnp.arange(SLOTS, dtype=jnp.int32), mode="drop")
    tap_rows = tap_frames[slot_of]
    weights = tap_weights[slot_of]
    summed = jnp.zeros((T_OUT, H, W, C), jnp.float32)
    for tap_index in range(TAPS):
        summed = summed + weights[:, tap_index, None, None, None] * source[tap_rows[:, tap_index]].astype(jnp.float32)
    blended = summed.astype(jnp.bfloat16)
    first_out = forward_block(blended, kernel_one, bias_one)
    second_out = forward_block(first_out, kernel_two, bias_two)
    picked = second_out[jnp.minimum(frame_of, T_OUT - 1)]
    decoded = jnp.where(in_use.reshape(-1)[:, None, None, None], picked, jnp.zeros((), jnp.bfloat16))
    incoming = upstream[slot_of]
    grad_mid = backward_block(incoming, first_out, kernel_two).astype(jnp.bfloat16)
    grad_low = backward_block(grad_mid, blended, kernel_one)
    source_grad = jnp.zeros((T_IN, H, W, C), jnp.float32)
    for tap_index in range(TAPS):
        source_grad = source_grad.at[tap_rows[:, tap_index]].add(weights[:, tap_index, None, None, None] * grad_low)
    return decoded, source_grad
```

```python
import jax
import jax.numpy as jnp
from jax import lax
from jax.experimental import pallas as pl
from jax.experimental.pallas import tpu as pltpu
from jax.sharding import PartitionSpec as P

MESH = pl.DeviceIdType.MESH
FRAMES = 4
CAP = 9
TAPS = 4
WINDOW = 16
BELOW = 6
W = 32
C = 256
OWN, NEAR, FAR = 0, 1, 2
BF16 = jnp.bfloat16
F32 = jnp.float32


def kernel(
    spans,
    lines,
    source,
    counts,
    frames,
    weights,
    kernel_one,
    bias_one,
    kernel_two,
    bias_two,
    upstream,
    decoded,
    source_grad,
    window,
    w_one,
    w_two,
    b_one,
    b_two,
    raw,
    blended,
    first,
    middle,
    low,
    back_two,
    parts,
    inc,
    act_one,
    grad_mid,
    act_two,
    inc_edge,
    act_one_edge,
    grad_mid_edge,
    act_two_edge,
    last,
    spread,
    arrived,
    total,
    result,
    mix,
    c_s,
    f_s,
    w_s,
    local,
    send,
    recv,
):
    d = lax.axis_index("tm")
    r = lax.axis_index("rows")
    odd = lax.rem(r, 2)
    near = r + 1 - 2 * odd
    far = lax.rem(r - 1 + 2 * odd + lines, lines)
    far_there = jnp.where(odd == 0, r > 0, r < lines - 1)
    near_tap = 2 - 2 * odd
    far_tap = 2 * odd

    def span(by):
        return lax.rem(d + by + spans, spans)

    reach = [(by, r) for by in (-2, -1, 1, 2)] + [(0, near), (0, far)]
    reach += [(by, row) for by in (-1, 1) for row in (near, far)]
    barrier = pltpu.get_barrier_semaphore()
    for by, row in reach:
        pl.semaphore_signal(
            barrier, inc=1, device_id={"tm": span(by), "rows": row}, device_id_type=MESH
        )

    def fetch(k, src, dst):
        copy = pltpu.make_async_copy(src, dst, local.at[k])
        copy.start()
        return copy

    get_source = fetch(0, source, window.at[pl.ds(BELOW, FRAMES)])
    get_counts = fetch(1, counts, c_s)
    get_frames = fetch(2, frames, f_s)
    get_weights = fetch(3, weights, w_s)
    get_raw = fetch(4, upstream, raw)
    get_two = fetch(5, kernel_two, w_two)
    get_one = fetch(6, kernel_one, w_one)
    get_b_one = fetch(7, bias_one, b_one)
    get_b_two = fetch(8, bias_two, b_two)

    copies = []

    def push(src, dst, by, row):
        k = len(copies)
        copy = pltpu.make_async_remote_copy(
            src_ref=src,
            dst_ref=dst,
            send_sem=send.at[k],
            recv_sem=recv.at[k],
            device_id={"tm": span(by), "rows": row},
            device_id_type=MESH,
        )
        copy.start()
        copies.append(copy)
        return copy

    def exchange(box, edge, ends):
        mine = box.at[OWN, pl.ds(1, CAP)]
        head = box.at[OWN, 1]
        return [
            push(mine, box.at[FAR, pl.ds(1, CAP)], 0, far),
            push(ends, box.at[FAR, 0], 1, far),
            push(head, edge.at[FAR], -1, far),
            push(ends, box.at[OWN, 0], 1, r),
            push(head, edge.at[OWN], -1, r),
            push(ends, box.at[NEAR, 0], 1, near),
            push(head, edge.at[NEAR], -1, near),
            push(mine, box.at[NEAR, pl.ds(1, CAP)], 0, near),
        ]

    get_source.wait()
    pl.semaphore_wait(barrier, len(reach))
    sources = [
        push(window.at[pl.ds(BELOW, 4)], window.at[pl.ds(2, 4)], 1, r),
        push(window.at[pl.ds(BELOW, 4)], window.at[pl.ds(10, 4)], -1, r),
        push(window.at[pl.ds(BELOW + 2, 2)], window.at[pl.ds(0, 2)], 2, r),
        push(window.at[pl.ds(BELOW, 2)], window.at[pl.ds(14, 2)], -2, r),
    ]

    get_counts.wait()
    get_frames.wait()
    get_weights.wait()
    filled = c_s[0]
    lowest = d * FRAMES - BELOW
    used = [j < filled for j in range(CAP)]
    none = jnp.zeros((W, C), BF16)

    get_raw.wait()
    for j in range(CAP):
        inc[OWN, 1 + j] = jnp.where(used[j], raw[j], none)
    last[0] = raw[jnp.clip(filled - 1, 0, CAP - 1)]
    inc_copies = exchange(inc, inc_edge, last.at[0])

    for j in range(CAP):
        for f in range(WINDOW):
            weight = jnp.float32(0.0)
            for k in range(TAPS):
                weight += jnp.where(f_s[j, k] == lowest + f, w_s[j, k], 0.0)
            mix[j, f] = jnp.where(used[j], weight, 0.0)

    for copy in sources:
        copy.wait_recv()
    for j in range(CAP):
        summed = jnp.zeros((W, C), F32)
        for k in range(TAPS):
            at = jnp.clip(f_s[j, k] - lowest, 0, WINDOW - 1)
            summed += w_s[j, k] * window[at].astype(F32)
        value = jnp.where(used[j], summed, 0.0).astype(BF16)
        blended[j] = value
        wide = value.astype(F32)
        value = (wide * jax.nn.sigmoid(wide)).astype(BF16)
        act_one[OWN, 1 + j] = value
        end = value if j == 0 else jnp.where(filled == j + 1, value, end)
    last[1] = end
    act_one_copies = exchange(act_one, act_one_edge, last.at[1])

    def settle(box, edge):
        for s in (OWN, NEAR, FAR):
            there = far_there if s == FAR else None
            before = d > 0 if there is None else (d > 0) & there
            after = d < spans - 1 if there is None else (d < spans - 1) & there
            box[s, 0] = jnp.where(before, box[s, 0], none)
            follow = jnp.where(after, edge[s], none)
            if s == FAR:
                box[s, 1] = jnp.where(there, box[s, 1], none)
            for e in range(2, CAP + 2):
                held = box[s, e] if e <= CAP else none
                if s == FAR:
                    held = jnp.where(there, held, none)
                box[s, e] = jnp.where(filled + 1 == e, follow, held)

    def convolve(box, w, back):
        taps = (1, near_tap, far_tap)
        for s in (OWN, NEAR, FAR):
            fields = jnp.concatenate(
                [box[s, a : a + CAP].reshape(CAP * W, C) for a in range(3)], axis=1
            )
            for c in range(3):
                if back:
                    tile = jnp.concatenate([w[2 - a, 2 - taps[s], 2 - c] for a in range(3)], axis=1)
                    dims = (((1,), (1,)), ((), ()))
                else:
                    tile = jnp.concatenate([w[a, taps[s], c] for a in range(3)], axis=0)
                    dims = (((1,), (0,)), ((), ()))
                term = lax.dot_general(fields, tile, dims, preferred_element_type=F32)
                if s == OWN:
                    parts[c] = term
                else:
                    parts[c] += term

    column = lax.broadcasted_iota(jnp.int32, (W, C), 0)

    def joined(j):
        rows = pl.ds(j * W, W)
        left = jnp.where(column == 0, 0.0, pltpu.roll(parts[0, rows], 1, 0))
        right = jnp.where(column == W - 1, 0.0, pltpu.roll(parts[2, rows], W - 1, 0))
        return parts[1, rows] + left + right

    for copy in inc_copies:
        copy.wait()
    settle(inc, inc_edge)
    get_two.wait()
    convolve(inc, w_two, True)
    for j in range(CAP):
        back_two[j] = joined(j)

    for copy in act_one_copies:
        copy.wait()
    settle(act_one, act_one_edge)
    get_one.wait()
    get_b_one.wait()
    get_b_two.wait()
    convolve(act_one, w_one, False)
    for j in range(CAP):
        value = blended[j].astype(F32) + joined(j) + b_one[...]
        value = jnp.where(used[j], value, 0.0).astype(BF16)
        first[j] = value
        wide = value.astype(F32)
        gate = jax.nn.sigmoid(wide)
        act = (wide * gate).astype(BF16)
        act_two[OWN, 1 + j] = act
        slope = gate * (1.0 + wide * (1.0 - gate))
        given = jnp.where(used[j], raw[j], none).astype(F32)
        value = given + slope * back_two[j]
        value = jnp.where(used[j], value, 0.0).astype(BF16)
        grad_mid[OWN, 1 + j] = value
        end_mid = value if j == 0 else jnp.where(filled == j + 1, value, end_mid)
        end_two = act if j == 0 else jnp.where(filled == j + 1, act, end_two)
    last[2] = end_mid
    grad_mid_copies = exchange(grad_mid, grad_mid_edge, last.at[2])
    last[3] = end_two
    act_two_copies = exchange(act_two, act_two_edge, last.at[3])

    for copy in grad_mid_copies:
        copy.wait()
    settle(grad_mid, grad_mid_edge)
    convolve(grad_mid, w_one, True)
    for j in range(CAP):
        wide = blended[j].astype(F32)
        gate = jax.nn.sigmoid(wide)
        slope = gate * (1.0 + wide * (1.0 - gate))
        low[j] = grad_mid[OWN, 1 + j].astype(F32) * jnp.where(used[j], 1.0, 0.0) + slope * joined(j)
    for f in range(WINDOW):
        summed = mix[0, f] * low[0]
        for j in range(1, CAP):
            summed += mix[j, f] * low[j]
        if BELOW <= f < BELOW + FRAMES:
            total[f - BELOW] = summed
        else:
            spread[f] = summed.astype(BF16)
    spread_copies = [
        push(spread.at[pl.ds(2, 4)], arrived.at[pl.ds(0, 4)], -1, r),
        push(spread.at[pl.ds(10, 4)], arrived.at[pl.ds(4, 4)], 1, r),
        push(spread.at[pl.ds(0, 2)], arrived.at[pl.ds(8, 2)], -2, r),
        push(spread.at[pl.ds(14, 2)], arrived.at[pl.ds(10, 2)], 2, r),
    ]

    for copy in act_two_copies:
        copy.wait()
    settle(act_two, act_two_edge)
    convolve(act_two, w_two, False)
    for j in range(CAP):
        value = first[j].astype(F32) + joined(j) + b_two[...]
        result[j] = jnp.where(used[j], value, 0.0).astype(BF16)
    put_decoded = fetch(9, result, decoded)

    for copy in spread_copies:
        copy.wait_recv()
    for f in range(FRAMES):
        value = total[f] + arrived[f].astype(F32) + arrived[4 + f].astype(F32)
        if f >= 2:
            value += arrived[8 + f - 2].astype(F32)
        else:
            value += arrived[10 + f].astype(F32)
        total[f] = value
    put_grad = fetch(10, total, source_grad)
    for copy in sources + spread_copies:
        copy.wait_send()
    put_decoded.wait()
    put_grad.wait()


def solution(mesh):
    spans, lines = mesh.shape["tm"], mesh.shape["rows"]

    def body(
        source,
        frame_counts,
        tap_frames,
        tap_weights,
        kernel_one,
        bias_one,
        kernel_two,
        bias_two,
        upstream,
    ):
        box = pltpu.VMEM((3, CAP + 2, W, C), BF16)
        edge = pltpu.VMEM((3, W, C), BF16)
        slots = pltpu.VMEM((CAP, W, C), BF16)
        wide_slots = pltpu.VMEM((CAP, W, C), F32)
        kernels = pltpu.VMEM((3, 3, 3, C, C), BF16)
        bias = pltpu.VMEM((1, C), F32)
        decoded, source_grad = pl.pallas_call(
            lambda *refs: kernel(spans, lines, *refs),
            out_shape=(
                jax.ShapeDtypeStruct((CAP, W, C), BF16),
                jax.ShapeDtypeStruct((FRAMES, W, C), F32),
            ),
            in_specs=[pl.BlockSpec(memory_space=pl.ANY)] * 9,
            out_specs=[pl.BlockSpec(memory_space=pl.ANY)] * 2,
            scratch_shapes=[
                pltpu.VMEM((WINDOW, W, C), BF16),
                kernels,
                kernels,
                bias,
                bias,
                slots,
                slots,
                slots,
                slots,
                wide_slots,
                wide_slots,
                pltpu.VMEM((3, CAP * W, C), F32),
                box,
                box,
                box,
                box,
                edge,
                edge,
                edge,
                edge,
                pltpu.VMEM((4, W, C), BF16),
                pltpu.VMEM((WINDOW, W, C), BF16),
                pltpu.VMEM((12, W, C), BF16),
                pltpu.VMEM((FRAMES, W, C), F32),
                slots,
                pltpu.SMEM((CAP, WINDOW), F32),
                pltpu.SMEM((1,), jnp.int32),
                pltpu.SMEM((CAP, TAPS), jnp.int32),
                pltpu.SMEM((CAP, TAPS), F32),
                pltpu.SemaphoreType.DMA((11,)),
                pltpu.SemaphoreType.DMA((40,)),
                pltpu.SemaphoreType.DMA((40,)),
            ],
            compiler_params=pltpu.CompilerParams(
                collective_id=0, has_side_effects=True, vmem_limit_bytes=48 * 1024 * 1024
            ),
            cost_estimate=pl.CostEstimate(
                flops=4 * 2 * CAP * W * 27 * C * C,
                bytes_accessed=2 * 27 * C * C * 2,
                transcendentals=0,
            ),
        )(
            source.reshape(FRAMES, W, C),
            frame_counts,
            tap_frames,
            tap_weights,
            kernel_one,
            bias_one.reshape(1, C),
            kernel_two,
            bias_two.reshape(1, C),
            upstream.reshape(CAP, W, C),
        )
        return decoded.reshape(CAP, 1, W, C), source_grad.reshape(FRAMES, 1, W, C)

    whole = P("tm", "rows", None, None)
    return jax.shard_map(
        body,
        mesh=mesh,
        in_specs=(whole, P("tm"), P("tm", None), P("tm", None), P(), P(), P(), P(), whole),
        out_specs=(whole, whole),
        check_vma=False,
    )
```

```python
import jax
import jax.numpy as jnp
from jax import lax
from jax.experimental import pallas as pl
from jax.experimental.pallas import tpu as pltpu
from jax.sharding import PartitionSpec as P

MESH = pl.DeviceIdType.MESH
FRAMES = 4
CAP = 9
TAPS = 4
WINDOW = 16
BELOW = 6
W = 32
C = 256
OWN, NEAR, FAR = 0, 1, 2
BF16 = jnp.bfloat16
F32 = jnp.float32


def kernel(
    spans,
    lines,
    source,
    counts,
    frames,
    weights,
    kernel_one,
    bias_one,
    kernel_two,
    bias_two,
    upstream,
    decoded,
    source_grad,
    window,
    w_one,
    w_two,
    b_one,
    b_two,
    raw,
    blended,
    first,
    low,
    back_two,
    slope_one,
    parts,
    inc,
    act_one,
    grad_mid,
    act_two,
    inc_edge,
    act_one_edge,
    grad_mid_edge,
    act_two_edge,
    last,
    spread,
    arrived,
    mix,
    c_s,
    f_s,
    w_s,
    local,
    send,
    recv,
):
    d = lax.axis_index("tm")
    r = lax.axis_index("rows")
    odd = lax.rem(r, 2)
    near = r + 1 - 2 * odd
    far = lax.rem(r - 1 + 2 * odd + lines, lines)
    far_there = jnp.where(odd == 0, r > 0, r < lines - 1)
    near_tap = 2 - 2 * odd
    far_tap = 2 * odd

    upper = spans - 1

    def exists(by):
        if by == 0:
            return None
        return d >= -by if by < 0 else d <= upper - by

    def both(one, two):
        if one is None or two is None:
            return two if one is None else one
        return one & two

    def when(condition, action):
        if condition is None:
            action()
        else:
            pl.when(condition)(action)

    def line(row):
        return far_there if row is far else None

    reach = [(by, r) for by in (-2, -1, 1, 2)] + [(0, near), (0, far)]
    reach += [(by, row) for by in (-1, 1) for row in (near, far)]
    barrier = pltpu.get_barrier_semaphore()
    greeted = jnp.int32(0)
    for by, row in reach:
        there = both(exists(by), line(row))

        def greet(by=by, row=row):
            pl.semaphore_signal(
                barrier, inc=1, device_id={"tm": d + by, "rows": row}, device_id_type=MESH
            )

        when(there, greet)
        greeted += 1 if there is None else jnp.where(there, 1, 0)

    def fetch(k, src, dst):
        copy = pltpu.make_async_copy(src, dst, local.at[k])
        copy.start()
        fetched.append(copy)
        return copy

    fetched = []
    get_source = fetch(0, source, window.at[pl.ds(BELOW, FRAMES)])
    get_raw = fetch(4, upstream, raw)
    get_counts = fetch(1, counts, c_s)
    get_frames = fetch(2, frames, f_s)
    get_weights = fetch(3, weights, w_s)
    get_two = fetch(5, kernel_two, w_two)
    get_one = fetch(6, kernel_one, w_one)
    get_b_one = fetch(7, bias_one, b_one)
    get_b_two = fetch(8, bias_two, b_two)

    copies = []

    def push(src, dst, by, row):
        k = len(copies)
        copy = pltpu.make_async_remote_copy(
            src_ref=src,
            dst_ref=dst,
            send_sem=send.at[k],
            recv_sem=recv.at[k],
            device_id={"tm": d + by, "rows": row},
            device_id_type=MESH,
        )
        when(both(exists(by), line(row)), copy.start)
        entry = [copy, both(exists(by), line(row)), both(exists(-by), line(row)), True, True]
        copies.append(entry)
        return entry

    def landed(*entries):
        for entry in entries:
            if entry[4]:
                when(entry[2], entry[0].wait_recv)
                entry[4] = False

    def left(*entries):
        for entry in entries:
            if entry[3]:
                when(entry[1], entry[0].wait_send)
                entry[3] = False

    def exchange(box, edge, ends):
        mine = box.at[OWN, pl.ds(1, CAP)]
        head = box.at[OWN, 1]
        far_last = push(ends, box.at[FAR, 0], 1, far)
        far_head = push(head, edge.at[FAR], -1, far)
        own_last = push(ends, box.at[OWN, 0], 1, r)
        own_head = push(head, edge.at[OWN], -1, r)
        far_mine = push(mine, box.at[FAR, pl.ds(1, CAP)], 0, far)
        near_last = push(ends, box.at[NEAR, 0], 1, near)
        near_head = push(head, edge.at[NEAR], -1, near)
        near_mine = push(mine, box.at[NEAR, pl.ds(1, CAP)], 0, near)
        out = (far_head, own_head, near_head, far_mine, near_mine)
        return (
            (own_last, own_head),
            (near_last, near_head, near_mine),
            (far_last, far_head, far_mine),
            out,
        )

    get_source.wait()
    pl.semaphore_wait(barrier, greeted)
    sources = [
        push(window.at[pl.ds(BELOW + 2, 2)], window.at[pl.ds(0, 2)], 2, r),
        push(window.at[pl.ds(BELOW, 2)], window.at[pl.ds(14, 2)], -2, r),
        push(window.at[pl.ds(BELOW, 4)], window.at[pl.ds(2, 4)], 1, r),
        push(window.at[pl.ds(BELOW, 4)], window.at[pl.ds(10, 4)], -1, r),
    ]

    get_counts.wait()
    filled = c_s[0]
    lowest = d * FRAMES - BELOW
    used = [j < filled for j in range(CAP)]
    none = jnp.zeros((W, C), BF16)

    get_raw.wait()
    for j in range(CAP):
        inc[OWN, 1 + j] = jnp.where(used[j], raw[j], none)
    last[0] = raw[jnp.clip(filled - 1, 0, CAP - 1)]
    inc_copies = exchange(inc, inc_edge, last.at[0])

    get_frames.wait()
    get_weights.wait()
    landed(*sources)
    for j in range(CAP):
        summed = jnp.zeros((W, C), F32)
        for k in range(TAPS):
            at = jnp.clip(f_s[k, j] - lowest, 0, WINDOW - 1)
            summed += w_s[k, j] * window[at].astype(F32)
        value = jnp.where(used[j], summed, 0.0).astype(BF16)
        blended[j] = value
        wide = value.astype(F32)
        value = (wide * jax.nn.sigmoid(wide)).astype(BF16)
        act_one[OWN, 1 + j] = value
        end = value if j == 0 else jnp.where(filled == j + 1, value, end)
    last[1] = end
    act_one_copies = exchange(act_one, act_one_edge, last.at[1])

    for j in range(CAP):
        for f in range(WINDOW):
            weight = jnp.float32(0.0)
            for k in range(TAPS):
                weight += jnp.where(f_s[k, j] == lowest + f, w_s[k, j], 0.0)
            mix[j, f] = jnp.where(used[j], weight, 0.0)

    def settle(s, box, edge):
        there = far_there if s == FAR else None
        before = both(exists(-1), there)
        after = both(exists(1), there)
        box[s, 0] = jnp.where(before, box[s, 0], none)
        follow = jnp.where(after, edge[s], none)
        if s == FAR:
            box[s, 1] = jnp.where(there, box[s, 1], none)
        for e in range(2, CAP + 2):
            held = box[s, e] if e <= CAP else none
            if s == FAR:
                held = jnp.where(there, held, none)
            box[s, e] = jnp.where(filled + 1 == e, follow, held)

    def convolve(copied, box, edge, w, back):
        taps = (1, near_tap, far_tap)
        left(*copied[3])
        for s in (OWN, NEAR, FAR):
            landed(*copied[s])
            settle(s, box, edge)
            fields = jnp.concatenate(
                [box[s, a : a + CAP].reshape(CAP * W, C) for a in range(3)], axis=1
            )
            for c in range(3):
                if back:
                    tile = jnp.concatenate([w[2 - a, 2 - taps[s], 2 - c] for a in range(3)], axis=1)
                    dims = (((1,), (1,)), ((), ()))
                else:
                    tile = jnp.concatenate([w[a, taps[s], c] for a in range(3)], axis=0)
                    dims = (((1,), (0,)), ((), ()))
                term = lax.dot_general(fields, tile, dims, preferred_element_type=F32)
                if s == OWN:
                    parts[c] = term
                else:
                    parts[c] += term

    column = lax.broadcasted_iota(jnp.int32, (W, C), 0)

    def joined(j):
        rows = pl.ds(j * W, W)
        before = jnp.where(column == 0, 0.0, pltpu.roll(parts[0, rows], 1, 0))
        after = jnp.where(column == W - 1, 0.0, pltpu.roll(parts[2, rows], W - 1, 0))
        return parts[1, rows] + before + after

    get_two.wait()
    convolve(inc_copies, inc, inc_edge, w_two, True)
    for j in range(CAP):
        back_two[j] = joined(j)

    get_one.wait()
    get_b_one.wait()
    get_b_two.wait()
    convolve(act_one_copies, act_one, act_one_edge, w_one, False)
    for j in range(CAP):
        value = blended[j].astype(F32) + joined(j) + b_one[...]
        value = jnp.where(used[j], value, 0.0).astype(BF16)
        first[j] = value
        wide = value.astype(F32)
        gate = jax.nn.sigmoid(wide)
        slope = gate * (1.0 + wide * (1.0 - gate))
        given = jnp.where(used[j], raw[j], none).astype(F32)
        value = given + slope * back_two[j]
        value = jnp.where(used[j], value, 0.0).astype(BF16)
        grad_mid[OWN, 1 + j] = value
        end_mid = value if j == 0 else jnp.where(filled == j + 1, value, end_mid)
    last[2] = end_mid
    grad_mid_copies = exchange(grad_mid, grad_mid_edge, last.at[2])
    for j in range(CAP):
        wide = first[j].astype(F32)
        act = (wide * jax.nn.sigmoid(wide)).astype(BF16)
        act_two[OWN, 1 + j] = act
        end_two = act if j == 0 else jnp.where(filled == j + 1, act, end_two)
        wide = blended[j].astype(F32)
        gate = jax.nn.sigmoid(wide)
        slope_one[j] = gate * (1.0 + wide * (1.0 - gate))
        low[j] = grad_mid[OWN, 1 + j].astype(F32)
    last[3] = end_two
    act_two_copies = exchange(act_two, act_two_edge, last.at[3])

    convolve(grad_mid_copies, grad_mid, grad_mid_edge, w_one, True)
    for j in range(CAP):
        low[j] += slope_one[j] * joined(j)

    def gathered(f):
        summed = mix[0, f] * low[0]
        for j in range(1, CAP):
            summed += mix[j, f] * low[j]
        return summed

    spread_copies = []
    for start, count, at, by in ((0, 2, 8, -2), (14, 2, 10, 2), (2, 4, 0, -1), (10, 4, 4, 1)):
        for f in range(start, start + count):
            spread[f] = gathered(f).astype(BF16)
        spread_copies.append(push(spread.at[pl.ds(start, count)], arrived.at[pl.ds(at, count)], by, r))
    for f in range(FRAMES):
        source_grad[f] = gathered(BELOW + f)

    convolve(act_two_copies, act_two, act_two_edge, w_two, False)
    for j in range(CAP):
        value = first[j].astype(F32) + joined(j) + b_two[...]
        decoded[j] = jnp.where(used[j], value, 0.0).astype(BF16)

    landed(*spread_copies)
    for f in range(FRAMES):
        value = source_grad[f]
        value += jnp.where(exists(1), arrived[f].astype(F32), 0.0)
        value += jnp.where(exists(-1), arrived[4 + f].astype(F32), 0.0)
        if f >= 2:
            value += jnp.where(exists(2), arrived[8 + f - 2].astype(F32), 0.0)
        else:
            value += jnp.where(exists(-2), arrived[10 + f].astype(F32), 0.0)
        source_grad[f] = value
    left(*copies)


def finish(decoded_in, grad_in, decoded, source_grad, done):
    one = pltpu.make_async_copy(decoded_in, decoded, done.at[0])
    two = pltpu.make_async_copy(grad_in, source_grad, done.at[1])
    one.start()
    two.start()
    one.wait()
    two.wait()


def solution(mesh):
    spans, lines = mesh.shape["tm"], mesh.shape["rows"]

    def body(
        source,
        frame_counts,
        tap_frames,
        tap_weights,
        kernel_one,
        bias_one,
        kernel_two,
        bias_two,
        upstream,
    ):
        box = pltpu.VMEM((3, CAP + 2, W, C), BF16)
        edge = pltpu.VMEM((3, W, C), BF16)
        slots = pltpu.VMEM((CAP, W, C), BF16)
        wide_slots = pltpu.VMEM((CAP, W, C), F32)
        kernels = pltpu.VMEM((3, 3, 3, C, C), BF16)
        bias = pltpu.VMEM((1, C), F32)
        decoded, source_grad = pl.pallas_call(
            lambda *refs: kernel(spans, lines, *refs),
            out_shape=(
                pltpu.VMEM((CAP, W, C), BF16),
                pltpu.VMEM((FRAMES, W, C), F32),
            ),
            in_specs=[pl.BlockSpec(memory_space=pl.ANY)] * 9,
            out_specs=[pl.BlockSpec(memory_space=pltpu.VMEM)] * 2,
            scratch_shapes=[
                pltpu.VMEM((WINDOW, W, C), BF16),
                kernels,
                kernels,
                bias,
                bias,
                slots,
                slots,
                slots,
                wide_slots,
                wide_slots,
                wide_slots,
                pltpu.VMEM((3, CAP * W, C), F32),
                box,
                box,
                box,
                box,
                edge,
                edge,
                edge,
                edge,
                pltpu.VMEM((4, W, C), BF16),
                pltpu.VMEM((WINDOW, W, C), BF16),
                pltpu.VMEM((12, W, C), BF16),
                pltpu.SMEM((CAP, WINDOW), F32),
                pltpu.SMEM((1,), jnp.int32),
                pltpu.SMEM((TAPS, CAP), jnp.int32),
                pltpu.SMEM((TAPS, CAP), F32),
                pltpu.SemaphoreType.DMA((9,)),
                pltpu.SemaphoreType.DMA((40,)),
                pltpu.SemaphoreType.DMA((40,)),
            ],
            compiler_params=pltpu.CompilerParams(
                collective_id=0, has_side_effects=True, vmem_limit_bytes=48 * 1024 * 1024
            ),
            cost_estimate=pl.CostEstimate(
                flops=4 * 2 * CAP * W * 27 * C * C,
                bytes_accessed=2 * 27 * C * C * 2,
                transcendentals=0,
            ),
        )(
            *(
                x if x is frame_counts else pltpu.with_memory_space_constraint(x, pltpu.HBM)
                for x in (
                    source.reshape(FRAMES, W, C),
                    frame_counts,
                    tap_frames.T,
                    tap_weights.T,
                    kernel_one,
                    bias_one.reshape(1, C),
                    kernel_two,
                    bias_two.reshape(1, C),
                    upstream.reshape(CAP, W, C),
                )
            )
        )
        decoded, source_grad = pl.pallas_call(
            finish,
            out_shape=(
                jax.ShapeDtypeStruct((CAP, W, C), BF16),
                jax.ShapeDtypeStruct((FRAMES, W, C), F32),
            ),
            in_specs=[pl.BlockSpec(memory_space=pltpu.VMEM)] * 2,
            out_specs=[pl.BlockSpec(memory_space=pl.ANY)] * 2,
            scratch_shapes=[pltpu.SemaphoreType.DMA((2,))],
        )(decoded, source_grad)
        return decoded.reshape(CAP, 1, W, C), source_grad.reshape(FRAMES, 1, W, C)

    whole = P("tm", "rows", None, None)
    return jax.shard_map(
        body,
        mesh=mesh,
        in_specs=(whole, P("tm"), P("tm", None), P("tm", None), P(), P(), P(), P(), whole),
        out_specs=(whole, whole),
        check_vma=False,
    )
```

```python
import jax
import jax.numpy as jnp
from jax import lax
from jax.experimental import pallas as pl
from jax.experimental.pallas import tpu as pltpu
from jax.sharding import PartitionSpec as P

MESH = pl.DeviceIdType.MESH
FRAMES = 4
CAP = 9
TAPS = 4
WINDOW = 16
BELOW = 6
W = 32
C = 256
OWN, NEAR, FAR = 0, 1, 2
BF16 = jnp.bfloat16
F32 = jnp.float32


def kernel(
    spans,
    lines,
    source,
    counts,
    frames,
    weights,
    kernel_one,
    bias_one,
    kernel_two,
    bias_two,
    upstream,
    decoded,
    source_grad,
    window,
    w_one,
    w_two,
    b_one,
    b_two,
    raw,
    blended,
    first,
    low,
    back_two,
    slope_one,
    parts,
    after,
    inc,
    act_one,
    grad_mid,
    act_two,
    inc_edge,
    act_one_edge,
    grad_mid_edge,
    act_two_edge,
    last,
    spread,
    arrived,
    mix,
    c_s,
    f_s,
    w_s,
    local,
    send,
    recv,
):
    d = lax.axis_index("tm")
    r = lax.axis_index("rows")
    odd = lax.rem(r, 2)
    near = r + 1 - 2 * odd
    far = lax.rem(r - 1 + 2 * odd + lines, lines)
    far_there = jnp.where(odd == 0, r > 0, r < lines - 1)
    near_tap = 2 - 2 * odd
    far_tap = 2 * odd

    upper = spans - 1

    def exists(by):
        if by == 0:
            return None
        return d >= -by if by < 0 else d <= upper - by

    def both(one, two):
        if one is None or two is None:
            return two if one is None else one
        return one & two

    def when(condition, action):
        if condition is None:
            action()
        else:
            pl.when(condition)(action)

    def line(row):
        return far_there if row is far else None

    reach = [(by, r) for by in (-2, -1, 1, 2)] + [(0, near), (0, far)]
    reach += [(by, row) for by in (-1, 1) for row in (near, far)]
    barrier = pltpu.get_barrier_semaphore()
    greeted = jnp.int32(0)
    for by, row in reach:
        there = both(exists(by), line(row))

        def greet(by=by, row=row):
            pl.semaphore_signal(
                barrier, inc=1, device_id={"tm": d + by, "rows": row}, device_id_type=MESH
            )

        when(there, greet)
        greeted += 1 if there is None else jnp.where(there, 1, 0)

    def fetch(k, src, dst):
        copy = pltpu.make_async_copy(src, dst, local.at[k])
        copy.start()
        fetched.append(copy)
        return copy

    fetched = []
    get_source = fetch(0, source, window.at[pl.ds(BELOW, FRAMES)])
    get_raw = fetch(4, upstream, raw)
    get_counts = fetch(1, counts, c_s)
    get_frames = fetch(2, frames, f_s)
    get_weights = fetch(3, weights, w_s)
    get_two = fetch(5, kernel_two, w_two)
    get_one = fetch(6, kernel_one, w_one)
    get_b_one = fetch(7, bias_one, b_one)
    get_b_two = fetch(8, bias_two, b_two)

    copies = []

    def push(src, dst, by, row):
        k = len(copies)
        copy = pltpu.make_async_remote_copy(
            src_ref=src,
            dst_ref=dst,
            send_sem=send.at[k],
            recv_sem=recv.at[k],
            device_id={"tm": d + by, "rows": row},
            device_id_type=MESH,
        )
        when(both(exists(by), line(row)), copy.start)
        entry = [copy, both(exists(by), line(row)), both(exists(-by), line(row)), True, True]
        copies.append(entry)
        return entry

    def landed(*entries):
        for entry in entries:
            if entry[4]:
                when(entry[2], entry[0].wait_recv)
                entry[4] = False

    def left(*entries):
        for entry in entries:
            if entry[3]:
                when(entry[1], entry[0].wait_send)
                entry[3] = False

    def exchange(box, edge, ends):
        mine = box.at[OWN, pl.ds(1, CAP)]
        head = box.at[OWN, 1]
        far_edges = push(ends, edge.at[0, FAR], 1, far), push(head, edge.at[1, FAR], -1, far)
        own_edges = push(ends, edge.at[0, OWN], 1, r), push(head, edge.at[1, OWN], -1, r)
        near_edges = push(ends, edge.at[0, NEAR], 1, near), push(head, edge.at[1, NEAR], -1, near)
        far_mine = push(mine, box.at[FAR, pl.ds(1, CAP)], 0, far)
        near_mine = push(mine, box.at[NEAR, pl.ds(1, CAP)], 0, near)
        return (None, near_mine, far_mine), (own_edges, near_edges, far_edges)

    get_source.wait()
    pl.semaphore_wait(barrier, greeted)
    sources = [
        push(window.at[pl.ds(BELOW + 2, 2)], window.at[pl.ds(0, 2)], 2, r),
        push(window.at[pl.ds(BELOW, 2)], window.at[pl.ds(14, 2)], -2, r),
        push(window.at[pl.ds(BELOW, 4)], window.at[pl.ds(2, 4)], 1, r),
        push(window.at[pl.ds(BELOW, 4)], window.at[pl.ds(10, 4)], -1, r),
    ]

    get_counts.wait()
    filled = c_s[0]
    lowest = d * FRAMES - BELOW
    used = [j < filled for j in range(CAP)]
    none = jnp.zeros((W, C), BF16)

    for box in (inc, act_one, grad_mid, act_two):
        for s in (OWN, NEAR, FAR):
            box[s, 0] = none
            box[s, CAP + 1] = none
    get_raw.wait()
    for j in range(CAP):
        inc[OWN, 1 + j] = jnp.where(used[j], raw[j], none)
    last[0] = raw[jnp.clip(filled - 1, 0, CAP - 1)]
    inc_copies = exchange(inc, inc_edge, last.at[0])

    get_frames.wait()
    get_weights.wait()
    landed(*sources)
    for j in range(CAP):
        summed = jnp.zeros((W, C), F32)
        for k in range(TAPS):
            at = jnp.clip(f_s[k, j] - lowest, 0, WINDOW - 1)
            summed += w_s[k, j] * window[at].astype(F32)
        value = jnp.where(used[j], summed, 0.0).astype(BF16)
        blended[j] = value
        wide = value.astype(F32)
        value = (wide * jax.nn.sigmoid(wide)).astype(BF16)
        act_one[OWN, 1 + j] = value
        end = value if j == 0 else jnp.where(filled == j + 1, value, end)
    last[1] = end
    act_one_copies = exchange(act_one, act_one_edge, last.at[1])

    for j in range(CAP):
        for f in range(WINDOW):
            weight = jnp.float32(0.0)
            for k in range(TAPS):
                weight += jnp.where(f_s[k, j] == lowest + f, w_s[k, j], 0.0)
            mix[j, f] = jnp.where(used[j], weight, 0.0)

    def products(fields, w, s, back, c, depths):
        tap = (1, near_tap, far_tap)[s]
        if back:
            tile = jnp.concatenate([w[2 - a, 2 - tap, 2 - c] for a in depths], axis=1)
            dims = (((1,), (1,)), ((), ()))
        else:
            tile = jnp.concatenate([w[a, tap, c] for a in depths], axis=0)
            dims = (((1,), (0,)), ((), ()))
        return lax.dot_general(fields, tile, dims, preferred_element_type=F32)

    def inner(copied, box, w, back, s):
        def step():
            if s != OWN:
                copied[0][s][0].wait_recv()
            fields = jnp.concatenate(
                [box[s, a : a + CAP].reshape(CAP * W, C) for a in range(3)], axis=1
            )
            for c in range(3):
                term = products(fields, w, s, back, c, (0, 1, 2))
                if s == OWN:
                    parts[c] = term
                else:
                    parts[c] += term

        when(far_there if s == FAR else None, step)
        if s != OWN:
            copied[0][s][4] = False

    def border(copied, edge, w, back, s):
        landed(*copied[1][s])
        there = far_there if s == FAR else None
        first_edge = jnp.where(both(exists(-1), there), edge[0, s], none)
        after_edge = jnp.where(both(exists(1), there), edge[1, s], none)
        for c in range(3):
            parts[c, :W] += products(first_edge, w, s, back, c, (0,))
            term = products(after_edge, w, s, back, c, (2,))
            if s == OWN:
                after[c] = term
            else:
                after[c] += term

    column = lax.broadcasted_iota(jnp.int32, (W, C), 0)

    def shifted(lower, centre, upper):
        lower = jnp.where(column == 0, 0.0, pltpu.roll(lower, 1, 0))
        upper = jnp.where(column == W - 1, 0.0, pltpu.roll(upper, W - 1, 0))
        return lower + centre + upper

    def joined():
        extra = shifted(after[0], after[1], after[2])
        for j in range(CAP):
            rows = pl.ds(j * W, W)
            value = shifted(parts[0, rows], parts[1, rows], parts[2, rows])
            yield j, value + jnp.where(filled == j + 1, extra, 0.0)

    def convolve(copied, box, edge, w, back):
        inner(copied, box, w, back, OWN)
        inner(copied, box, w, back, NEAR)
        border(copied, edge, w, back, OWN)
        border(copied, edge, w, back, NEAR)
        inner(copied, box, w, back, FAR)
        border(copied, edge, w, back, FAR)

    get_two.wait()
    convolve(inc_copies, inc, inc_edge, w_two, True)
    for j, value in joined():
        back_two[j] = value

    get_one.wait()
    get_b_one.wait()
    get_b_two.wait()
    convolve(act_one_copies, act_one, act_one_edge, w_one, False)
    for j, value in joined():
        value += blended[j].astype(F32) + b_one[...]
        value = jnp.where(used[j], value, 0.0).astype(BF16)
        first[j] = value
        wide = value.astype(F32)
        gate = jax.nn.sigmoid(wide)
        slope = gate * (1.0 + wide * (1.0 - gate))
        given = jnp.where(used[j], raw[j], none).astype(F32)
        value = given + slope * back_two[j]
        value = jnp.where(used[j], value, 0.0).astype(BF16)
        grad_mid[OWN, 1 + j] = value
        end_mid = value if j == 0 else jnp.where(filled == j + 1, value, end_mid)
    last[2] = end_mid
    grad_mid_copies = exchange(grad_mid, grad_mid_edge, last.at[2])
    for j in range(CAP):
        wide = first[j].astype(F32)
        act = (wide * jax.nn.sigmoid(wide)).astype(BF16)
        act_two[OWN, 1 + j] = act
        end_two = act if j == 0 else jnp.where(filled == j + 1, act, end_two)
        wide = blended[j].astype(F32)
        gate = jax.nn.sigmoid(wide)
        slope_one[j] = gate * (1.0 + wide * (1.0 - gate))
        low[j] = grad_mid[OWN, 1 + j].astype(F32)
    last[3] = end_two
    act_two_copies = exchange(act_two, act_two_edge, last.at[3])

    convolve(grad_mid_copies, grad_mid, grad_mid_edge, w_one, True)
    for j, value in joined():
        low[j] += slope_one[j] * value

    def gathered(f):
        summed = mix[0, f] * low[0]
        for j in range(1, CAP):
            summed += mix[j, f] * low[j]
        return summed

    spread_copies = []
    for start, count, at, by in ((0, 2, 8, -2), (14, 2, 10, 2), (2, 4, 0, -1), (10, 4, 4, 1)):
        for f in range(start, start + count):
            spread[f] = gathered(f).astype(BF16)
        spread_copies.append(push(spread.at[pl.ds(start, count)], arrived.at[pl.ds(at, count)], by, r))
    for f in range(FRAMES):
        source_grad[f] = gathered(BELOW + f)

    convolve(act_two_copies, act_two, act_two_edge, w_two, False)
    for j, value in joined():
        value += first[j].astype(F32) + b_two[...]
        decoded[j] = jnp.where(used[j], value, 0.0).astype(BF16)

    landed(*spread_copies)
    for f in range(FRAMES):
        value = source_grad[f]
        value += jnp.where(exists(1), arrived[f].astype(F32), 0.0)
        value += jnp.where(exists(-1), arrived[4 + f].astype(F32), 0.0)
        if f >= 2:
            value += jnp.where(exists(2), arrived[8 + f - 2].astype(F32), 0.0)
        else:
            value += jnp.where(exists(-2), arrived[10 + f].astype(F32), 0.0)
        source_grad[f] = value
    left(*copies)


def finish(decoded_in, grad_in, decoded, source_grad, done):
    one = pltpu.make_async_copy(decoded_in, decoded, done.at[0])
    two = pltpu.make_async_copy(grad_in, source_grad, done.at[1])
    one.start()
    two.start()
    one.wait()
    two.wait()


def solution(mesh):
    spans, lines = mesh.shape["tm"], mesh.shape["rows"]

    def body(
        source,
        frame_counts,
        tap_frames,
        tap_weights,
        kernel_one,
        bias_one,
        kernel_two,
        bias_two,
        upstream,
    ):
        box = pltpu.VMEM((3, CAP + 2, W, C), BF16)
        edge = pltpu.VMEM((2, 3, W, C), BF16)
        slots = pltpu.VMEM((CAP, W, C), BF16)
        wide_slots = pltpu.VMEM((CAP, W, C), F32)
        kernels = pltpu.VMEM((3, 3, 3, C, C), BF16)
        bias = pltpu.VMEM((1, C), F32)
        decoded, source_grad = pl.pallas_call(
            lambda *refs: kernel(spans, lines, *refs),
            out_shape=(
                pltpu.VMEM((CAP, W, C), BF16),
                pltpu.VMEM((FRAMES, W, C), F32),
            ),
            in_specs=[pl.BlockSpec(memory_space=pl.ANY)] * 9,
            out_specs=[pl.BlockSpec(memory_space=pltpu.VMEM)] * 2,
            scratch_shapes=[
                pltpu.VMEM((WINDOW, W, C), BF16),
                kernels,
                kernels,
                bias,
                bias,
                slots,
                slots,
                slots,
                wide_slots,
                wide_slots,
                wide_slots,
                pltpu.VMEM((3, CAP * W, C), F32),
                pltpu.VMEM((3, W, C), F32),
                box,
                box,
                box,
                box,
                edge,
                edge,
                edge,
                edge,
                pltpu.VMEM((4, W, C), BF16),
                pltpu.VMEM((WINDOW, W, C), BF16),
                pltpu.VMEM((12, W, C), BF16),
                pltpu.SMEM((CAP, WINDOW), F32),
                pltpu.SMEM((1,), jnp.int32),
                pltpu.SMEM((TAPS, CAP), jnp.int32),
                pltpu.SMEM((TAPS, CAP), F32),
                pltpu.SemaphoreType.DMA((9,)),
                pltpu.SemaphoreType.DMA((40,)),
                pltpu.SemaphoreType.DMA((40,)),
            ],
            compiler_params=pltpu.CompilerParams(
                collective_id=0, has_side_effects=True, vmem_limit_bytes=48 * 1024 * 1024
            ),
            cost_estimate=pl.CostEstimate(
                flops=4 * 2 * CAP * W * 27 * C * C,
                bytes_accessed=2 * 27 * C * C * 2,
                transcendentals=0,
            ),
        )(
            *(
                x if x is frame_counts else pltpu.with_memory_space_constraint(x, pltpu.HBM)
                for x in (
                    source.reshape(FRAMES, W, C),
                    frame_counts,
                    tap_frames.T,
                    tap_weights.T,
                    kernel_one,
                    bias_one.reshape(1, C),
                    kernel_two,
                    bias_two.reshape(1, C),
                    upstream.reshape(CAP, W, C),
                )
            )
        )
        decoded, source_grad = pl.pallas_call(
            finish,
            out_shape=(
                jax.ShapeDtypeStruct((CAP, W, C), BF16),
                jax.ShapeDtypeStruct((FRAMES, W, C), F32),
            ),
            in_specs=[pl.BlockSpec(memory_space=pltpu.VMEM)] * 2,
            out_specs=[pl.BlockSpec(memory_space=pl.ANY)] * 2,
            scratch_shapes=[pltpu.SemaphoreType.DMA((2,))],
        )(*(pltpu.with_memory_space_constraint(x, pltpu.VMEM) for x in (decoded, source_grad)))
        return decoded.reshape(CAP, 1, W, C), source_grad.reshape(FRAMES, 1, W, C)

    whole = P("tm", "rows", None, None)
    return jax.shard_map(
        body,
        mesh=mesh,
        in_specs=(whole, P("tm"), P("tm", None), P("tm", None), P(), P(), P(), P(), whole),
        out_specs=(whole, whole),
        check_vma=False,
    )
```

```python
import jax
import jax.numpy as jnp
from jax import lax
from jax.experimental import pallas as pl
from jax.experimental.pallas import tpu as pltpu
from jax.sharding import PartitionSpec as P

MESH = pl.DeviceIdType.MESH
FRAMES = 4
CAP = 9
TAPS = 4
WINDOW = 16
BELOW = 6
W = 32
C = 256
OWN, NEAR, FAR = 0, 1, 2
BF16 = jnp.bfloat16
F32 = jnp.float32


def kernel(
    spans,
    lines,
    source,
    counts,
    frames,
    weights,
    kernel_one,
    bias_one,
    kernel_two,
    bias_two,
    upstream,
    decoded,
    source_grad,
    window,
    w_one,
    w_two,
    b_one,
    b_two,
    raw,
    blended,
    first,
    low,
    back_two,
    slope_one,
    parts,
    after,
    inc,
    act_one,
    grad_mid,
    act_two,
    inc_edge,
    act_one_edge,
    grad_mid_edge,
    act_two_edge,
    last,
    spread,
    arrived,
    mix,
    c_s,
    f_s,
    w_s,
    local,
    send,
    recv,
):
    d = lax.axis_index("tm")
    r = lax.axis_index("rows")
    odd = lax.rem(r, 2)
    near = r + 1 - 2 * odd
    far = lax.rem(r - 1 + 2 * odd + lines, lines)
    far_there = jnp.where(odd == 0, r > 0, r < lines - 1)
    near_tap = 2 - 2 * odd
    far_tap = 2 * odd

    upper = spans - 1

    def exists(by):
        if by == 0:
            return None
        return d >= -by if by < 0 else d <= upper - by

    def both(one, two):
        if one is None or two is None:
            return two if one is None else one
        return one & two

    def when(condition, action):
        if condition is None:
            action()
        else:
            pl.when(condition)(action)

    def line(row):
        return far_there if row is far else None

    reach = [(by, r) for by in (-2, -1, 1, 2)] + [(0, near), (0, far)]
    barrier = pltpu.get_barrier_semaphore()
    greeted = jnp.int32(0)
    for by, row in reach:
        there = both(exists(by), line(row))

        def greet(by=by, row=row):
            pl.semaphore_signal(
                barrier, inc=1, device_id={"tm": d + by, "rows": row}, device_id_type=MESH
            )

        when(there, greet)
        greeted += 1 if there is None else jnp.where(there, 1, 0)

    def fetch(k, src, dst):
        copy = pltpu.make_async_copy(src, dst, local.at[k])
        copy.start()
        fetched.append(copy)
        return copy

    fetched = []
    get_source = fetch(0, source, window.at[pl.ds(BELOW, FRAMES)])
    get_raw = fetch(4, upstream, raw)
    get_counts = fetch(1, counts, c_s)
    get_frames = fetch(2, frames, f_s)
    get_weights = fetch(3, weights, w_s)
    get_two = fetch(5, kernel_two, w_two)
    get_one = fetch(6, kernel_one, w_one)
    get_b_one = fetch(7, bias_one, b_one)
    get_b_two = fetch(8, bias_two, b_two)

    copies = []

    def push(src, dst, by, row, held=None):
        k = len(copies)
        copy = pltpu.make_async_remote_copy(
            src_ref=src,
            dst_ref=dst,
            send_sem=send.at[k],
            recv_sem=recv.at[k],
            device_id={"tm": d + by, "rows": row},
            device_id_type=MESH,
        )
        sent = both(both(exists(by), line(row)), held)
        when(sent, copy.start)
        entry = [copy, sent, both(both(exists(-by), line(row)), held), True, True]
        copies.append(entry)
        return entry

    def landed(*entries):
        for entry in entries:
            if entry[4]:
                when(entry[2], entry[0].wait_recv)
                entry[4] = False

    def left(*entries):
        for entry in entries:
            if entry[3]:
                when(entry[1], entry[0].wait_send)
                entry[3] = False

    def send_edges(box, edge, ends):
        head = box.at[OWN, 1]
        far_edges = push(ends, edge.at[0, FAR], 1, far), push(head, edge.at[1, FAR], -1, far)
        own_edges = push(ends, edge.at[0, OWN], 1, r), push(head, edge.at[1, OWN], -1, r)
        near_edges = push(ends, edge.at[0, NEAR], 1, near), push(head, edge.at[1, NEAR], -1, near)
        return own_edges, near_edges, far_edges

    def send_slots(box):
        mine = box.at[OWN, pl.ds(1, CAP)]
        far_mine = push(mine, box.at[FAR, pl.ds(1, CAP)], 0, far)
        near_mine = push(mine, box.at[NEAR, pl.ds(1, CAP)], 0, near)
        return None, near_mine, far_mine

    get_source.wait()
    pl.semaphore_wait(barrier, greeted)
    sources = [
        push(window.at[pl.ds(BELOW + 2, 2)], window.at[pl.ds(0, 2)], 2, r),
        push(window.at[pl.ds(BELOW, 2)], window.at[pl.ds(14, 2)], -2, r),
        push(window.at[pl.ds(BELOW, 4)], window.at[pl.ds(2, 4)], 1, r),
        push(window.at[pl.ds(BELOW, 4)], window.at[pl.ds(10, 4)], -1, r),
    ]

    get_counts.wait()
    filled = c_s[0]
    lowest = d * FRAMES - BELOW
    used = [j < filled for j in range(CAP)]
    none = jnp.zeros((W, C), BF16)

    for box in (inc, act_one, grad_mid, act_two):
        for s in (OWN, NEAR, FAR):
            box[s, 0] = none
            box[s, CAP + 1] = none
    get_raw.wait()
    for j in range(CAP):
        inc[OWN, 1 + j] = jnp.where(used[j], raw[j], none)

    end = jnp.clip(filled - 1, 0, CAP - 1)
    last[0] = raw[end]
    inc_slots = send_slots(inc)
    edges = (
        push(last.at[0], inc_edge.at[0, OWN], 1, r),
        push(inc.at[OWN, 1], inc_edge.at[1, OWN], -1, r),
    )
    inc_edges = [edges]
    get_frames.wait()
    get_weights.wait()
    landed(*edges)
    for s, row in ((NEAR, near), (FAR, far)):
        inc_edges.append(
            [
                push(inc_edge.at[k, OWN], inc_edge.at[k, s], 0, row, exists((-1, 1)[k]))
                for k in range(2)
            ]
        )
    landed(*sources)

    def blend(j):
        summed = jnp.zeros((W, C), F32)
        for k in range(TAPS):
            at = jnp.clip(f_s[k, j] - lowest, 0, WINDOW - 1)
            summed += w_s[k, j] * window[at].astype(F32)
        return summed.astype(BF16)

    def silu(value):
        wide = value.astype(F32)
        return (wide * jax.nn.sigmoid(wide)).astype(BF16)

    value = blend(0)
    blended[0] = value
    act_one[OWN, 1] = silu(value)
    last[1] = silu(blend(end))
    act_one_edges = send_edges(act_one, act_one_edge, last.at[1])
    for j in range(1, CAP):
        value = jnp.where(used[j], blend(j), none)
        blended[j] = value
        act_one[OWN, 1 + j] = silu(value)
    act_one_slots = send_slots(act_one)

    def products(fields, w, s, back, c, depths):
        tap = (1, near_tap, far_tap)[s]
        if back:
            tile = jnp.concatenate([w[2 - a, 2 - tap, 2 - c] for a in depths], axis=1)
            dims = (((1,), (1,)), ((), ()))
        else:
            tile = jnp.concatenate([w[a, tap, c] for a in depths], axis=0)
            dims = (((1,), (0,)), ((), ()))
        return lax.dot_general(fields, tile, dims, preferred_element_type=F32)

    def inner(slots, box, w, back, s):
        def step():
            if s != OWN:
                slots[s][0].wait_recv()
            fields = jnp.concatenate(
                [box[s, a : a + CAP].reshape(CAP * W, C) for a in range(3)], axis=1
            )
            for c in range(3):
                term = products(fields, w, s, back, c, (0, 1, 2))
                if s == OWN:
                    parts[c] = term.reshape(CAP, W, C)
                else:
                    parts[c] += term.reshape(CAP, W, C)

        when(far_there if s == FAR else None, step)
        if s != OWN:
            slots[s][4] = False

    def border(edges, edge, w, back, s):
        landed(*edges[s])
        there = far_there if s == FAR else None
        first_edge = jnp.where(both(exists(-1), there), edge[0, s], none)
        after_edge = jnp.where(both(exists(1), there), edge[1, s], none)
        for c in range(3):
            parts[c, 0] += products(first_edge, w, s, back, c, (0,))
            term = products(after_edge, w, s, back, c, (2,))
            if s == OWN:
                after[c] = term
            else:
                after[c] += term

    column = lax.broadcasted_iota(jnp.int32, (W, C), 0)

    def shifted(lower, centre, upper):
        lower = jnp.where(column == 0, 0.0, pltpu.roll(lower, 1, 0))
        upper = jnp.where(column == W - 1, 0.0, pltpu.roll(upper, W - 1, 0))
        return lower + centre + upper

    def slot(j):
        return shifted(parts[0, j], parts[1, j], parts[2, j])

    def joined(extra, j):
        return slot(j) + jnp.where(filled == j + 1, extra, 0.0)

    def convolve(slots, edges, box, edge, w, back):
        for s in (OWN, NEAR, FAR):
            inner(slots, box, w, back, s)
        for s in (OWN, NEAR, FAR):
            border(edges, edge, w, back, s)
        return shifted(after[0], after[1], after[2])

    get_two.wait()
    extra = convolve(inc_slots, inc_edges, inc, inc_edge, w_two, True)
    for j in range(CAP):
        back_two[j] = joined(extra, j)

    get_one.wait()
    get_b_one.wait()
    get_b_two.wait()
    extra = convolve(act_one_slots, act_one_edges, act_one, act_one_edge, w_one, False)

    def first_at(j, conv):
        return (conv + blended[j].astype(F32) + b_one[...]).astype(BF16)

    def grad_at(j, value):
        wide = value.astype(F32)
        gate = jax.nn.sigmoid(wide)
        slope = gate * (1.0 + wide * (1.0 - gate))
        return (raw[j].astype(F32) + slope * back_two[j]).astype(BF16)

    value = first_at(0, joined(extra, 0))
    first[0] = value
    grad_mid[OWN, 1] = grad_at(0, value)
    value = first_at(end, slot(end) + extra)
    last[2] = grad_at(end, value)
    grad_mid_edges = send_edges(grad_mid, grad_mid_edge, last.at[2])
    last[3] = silu(value)
    for j in range(1, CAP):
        value = jnp.where(used[j], first_at(j, joined(extra, j)), none)
        first[j] = value
        grad_mid[OWN, 1 + j] = jnp.where(used[j], grad_at(j, value), none)
    grad_mid_slots = send_slots(grad_mid)
    for j in range(CAP):
        act_two[OWN, 1 + j] = silu(first[j])
    act_two_edges = send_edges(act_two, act_two_edge, last.at[3])
    act_two_slots = send_slots(act_two)
    for j in range(CAP):
        wide = blended[j].astype(F32)
        gate = jax.nn.sigmoid(wide)
        slope_one[j] = gate * (1.0 + wide * (1.0 - gate))
        for f in range(WINDOW):
            weight = jnp.float32(0.0)
            for k in range(TAPS):
                weight += jnp.where(f_s[k, j] == lowest + f, w_s[k, j], 0.0)
            mix[j, f] = jnp.where(used[j], weight, 0.0)

    extra = convolve(grad_mid_slots, grad_mid_edges, grad_mid, grad_mid_edge, w_one, True)
    for j in range(CAP):
        low[j] = grad_mid[OWN, 1 + j].astype(F32) + slope_one[j] * joined(extra, j)

    def gathered(f):
        summed = mix[0, f] * low[0]
        for j in range(1, CAP):
            summed += mix[j, f] * low[j]
        return summed

    spread_copies = []
    for start, count, at, by in ((0, 2, 8, -2), (14, 2, 10, 2), (2, 4, 0, -1), (10, 4, 4, 1)):
        for f in range(start, start + count):
            spread[f] = gathered(f).astype(BF16)
        spread_copies.append(push(spread.at[pl.ds(start, count)], arrived.at[pl.ds(at, count)], by, r))
    for f in range(FRAMES):
        source_grad[f] = gathered(BELOW + f)

    extra = convolve(act_two_slots, act_two_edges, act_two, act_two_edge, w_two, False)
    for j in range(CAP):
        value = joined(extra, j) + first[j].astype(F32) + b_two[...]
        decoded[j] = jnp.where(used[j], value, 0.0).astype(BF16)

    landed(*spread_copies)
    for f in range(FRAMES):
        value = source_grad[f]
        value += jnp.where(exists(1), arrived[f].astype(F32), 0.0)
        value += jnp.where(exists(-1), arrived[4 + f].astype(F32), 0.0)
        if f >= 2:
            value += jnp.where(exists(2), arrived[8 + f - 2].astype(F32), 0.0)
        else:
            value += jnp.where(exists(-2), arrived[10 + f].astype(F32), 0.0)
        source_grad[f] = value
    left(*copies)


def finish(decoded_in, grad_in, decoded, source_grad, done):
    one = pltpu.make_async_copy(decoded_in, decoded, done.at[0])
    two = pltpu.make_async_copy(grad_in, source_grad, done.at[1])
    one.start()
    two.start()
    one.wait()
    two.wait()


def solution(mesh):
    spans, lines = mesh.shape["tm"], mesh.shape["rows"]

    def body(
        source,
        frame_counts,
        tap_frames,
        tap_weights,
        kernel_one,
        bias_one,
        kernel_two,
        bias_two,
        upstream,
    ):
        box = pltpu.VMEM((3, CAP + 2, W, C), BF16)
        edge = pltpu.VMEM((2, 3, W, C), BF16)
        slots = pltpu.VMEM((CAP, W, C), BF16)
        wide_slots = pltpu.VMEM((CAP, W, C), F32)
        kernels = pltpu.VMEM((3, 3, 3, C, C), BF16)
        bias = pltpu.VMEM((1, C), F32)
        decoded, source_grad = pl.pallas_call(
            lambda *refs: kernel(spans, lines, *refs),
            out_shape=(
                pltpu.VMEM((CAP, W, C), BF16),
                pltpu.VMEM((FRAMES, W, C), F32),
            ),
            in_specs=[pl.BlockSpec(memory_space=pl.ANY)] * 9,
            out_specs=[pl.BlockSpec(memory_space=pltpu.VMEM)] * 2,
            scratch_shapes=[
                pltpu.VMEM((WINDOW, W, C), BF16),
                kernels,
                kernels,
                bias,
                bias,
                slots,
                slots,
                slots,
                wide_slots,
                wide_slots,
                wide_slots,
                pltpu.VMEM((3, CAP, W, C), F32),
                pltpu.VMEM((3, W, C), F32),
                box,
                box,
                box,
                box,
                edge,
                edge,
                edge,
                edge,
                pltpu.VMEM((4, W, C), BF16),
                pltpu.VMEM((WINDOW, W, C), BF16),
                pltpu.VMEM((12, W, C), BF16),
                pltpu.SMEM((CAP, WINDOW), F32),
                pltpu.SMEM((1,), jnp.int32),
                pltpu.SMEM((TAPS, CAP), jnp.int32),
                pltpu.SMEM((TAPS, CAP), F32),
                pltpu.SemaphoreType.DMA((9,)),
                pltpu.SemaphoreType.DMA((40,)),
                pltpu.SemaphoreType.DMA((40,)),
            ],
            compiler_params=pltpu.CompilerParams(
                collective_id=0, has_side_effects=True, vmem_limit_bytes=48 * 1024 * 1024
            ),
            cost_estimate=pl.CostEstimate(
                flops=4 * 2 * CAP * W * 27 * C * C,
                bytes_accessed=2 * 27 * C * C * 2,
                transcendentals=0,
            ),
        )(
            *(
                x if x is frame_counts else pltpu.with_memory_space_constraint(x, pltpu.HBM)
                for x in (
                    source.reshape(FRAMES, W, C),
                    frame_counts,
                    tap_frames.T,
                    tap_weights.T,
                    kernel_one,
                    bias_one.reshape(1, C),
                    kernel_two,
                    bias_two.reshape(1, C),
                    upstream.reshape(CAP, W, C),
                )
            )
        )
        decoded, source_grad = pl.pallas_call(
            finish,
            out_shape=(
                jax.ShapeDtypeStruct((CAP, W, C), BF16),
                jax.ShapeDtypeStruct((FRAMES, W, C), F32),
            ),
            in_specs=[pl.BlockSpec(memory_space=pltpu.VMEM)] * 2,
            out_specs=[pl.BlockSpec(memory_space=pl.ANY)] * 2,
            scratch_shapes=[pltpu.SemaphoreType.DMA((2,))],
        )(*(pltpu.with_memory_space_constraint(x, pltpu.VMEM) for x in (decoded, source_grad)))
        return decoded.reshape(CAP, 1, W, C), source_grad.reshape(FRAMES, 1, W, C)

    whole = P("tm", "rows", None, None)
    return jax.shard_map(
        body,
        mesh=mesh,
        in_specs=(whole, P("tm"), P("tm", None), P("tm", None), P(), P(), P(), P(), whole),
        out_specs=(whole, whole),
        check_vma=False,
    )
```

```python
import jax
import jax.numpy as jnp
from jax import lax
from jax.experimental import pallas as pl
from jax.experimental.pallas import tpu as pltpu
from jax.sharding import PartitionSpec as P

MESH = pl.DeviceIdType.MESH
FRAMES = 4
CAP = 9
TAPS = 4
WINDOW = 16
BELOW = 6
W = 32
C = 256
OWN, NEAR, FAR = 0, 1, 2
BF16 = jnp.bfloat16
F32 = jnp.float32


def kernel(
    spans,
    lines,
    source,
    counts,
    frames,
    weights,
    kernel_one,
    bias_one,
    kernel_two,
    bias_two,
    upstream,
    decoded,
    source_grad,
    window,
    w_one,
    w_two,
    b_one,
    b_two,
    raw,
    blended,
    first,
    low,
    back_two,
    slope_one,
    parts,
    after,
    inc,
    act_one,
    grad_mid,
    act_two,
    inc_edge,
    act_one_edge,
    grad_mid_edge,
    act_two_edge,
    last,
    spread,
    arrived,
    mix,
    c_s,
    f_s,
    w_s,
    local,
    send,
    recv,
):
    d = lax.axis_index("tm")
    r = lax.axis_index("rows")
    odd = lax.rem(r, 2)
    near = r + 1 - 2 * odd
    far = lax.rem(r - 1 + 2 * odd + lines, lines)
    far_there = jnp.where(odd == 0, r > 0, r < lines - 1)
    near_tap = 2 - 2 * odd
    far_tap = 2 * odd

    upper = spans - 1

    def exists(by):
        if by == 0:
            return None
        return d >= -by if by < 0 else d <= upper - by

    def both(one, two):
        if one is None or two is None:
            return two if one is None else one
        return one & two

    def when(condition, action):
        if condition is None:
            action()
        else:
            pl.when(condition)(action)

    def line(row):
        return far_there if row is far else None

    reach = [(by, r) for by in (-2, -1, 1, 2)] + [(0, near), (0, far)]
    barrier = pltpu.get_barrier_semaphore()
    greeted = jnp.int32(0)
    for by, row in reach:
        there = both(exists(by), line(row))

        def greet(by=by, row=row):
            pl.semaphore_signal(
                barrier, inc=1, device_id={"tm": d + by, "rows": row}, device_id_type=MESH
            )

        when(there, greet)
        greeted += 1 if there is None else jnp.where(there, 1, 0)

    def fetch(k, src, dst):
        copy = pltpu.make_async_copy(src, dst, local.at[k])
        copy.start()
        fetched.append(copy)
        return copy

    fetched = []
    get_source = fetch(0, source, window.at[pl.ds(BELOW, FRAMES)])
    get_raw = fetch(4, upstream, raw)
    get_counts = fetch(1, counts, c_s)
    get_frames = fetch(2, frames, f_s)
    get_weights = fetch(3, weights, w_s)
    get_two = fetch(5, kernel_two, w_two)
    get_one = fetch(6, kernel_one, w_one)
    get_b_one = fetch(7, bias_one, b_one)
    get_b_two = fetch(8, bias_two, b_two)

    copies = []

    def push(src, dst, by, row, held=None):
        k = len(copies)
        copy = pltpu.make_async_remote_copy(
            src_ref=src,
            dst_ref=dst,
            send_sem=send.at[k],
            recv_sem=recv.at[k],
            device_id={"tm": d + by, "rows": row},
            device_id_type=MESH,
        )
        sent = both(both(exists(by), line(row)), held)
        when(sent, copy.start)
        entry = [copy, sent, both(both(exists(-by), line(row)), held), True, True]
        copies.append(entry)
        return entry

    def landed(*entries):
        for entry in entries:
            if entry[4]:
                when(entry[2], entry[0].wait_recv)
                entry[4] = False

    def left(*entries):
        for entry in entries:
            if entry[3]:
                when(entry[1], entry[0].wait_send)
                entry[3] = False

    def send_edges(box, edge, ends):
        head = box.at[OWN, 1]
        far_edges = push(ends, edge.at[0, FAR], 1, far), push(head, edge.at[1, FAR], -1, far)
        own_edges = push(ends, edge.at[0, OWN], 1, r), push(head, edge.at[1, OWN], -1, r)
        near_edges = push(ends, edge.at[0, NEAR], 1, near), push(head, edge.at[1, NEAR], -1, near)
        return own_edges, near_edges, far_edges

    def send_slots(box):
        mine = box.at[OWN, pl.ds(1, CAP)]
        far_mine = push(mine, box.at[FAR, pl.ds(1, CAP)], 0, far)
        near_mine = push(mine, box.at[NEAR, pl.ds(1, CAP)], 0, near)
        return None, near_mine, far_mine

    get_source.wait()
    pl.semaphore_wait(barrier, greeted)
    sources = [
        push(window.at[pl.ds(BELOW + 2, 2)], window.at[pl.ds(0, 2)], 2, r),
        push(window.at[pl.ds(BELOW, 2)], window.at[pl.ds(14, 2)], -2, r),
        push(window.at[pl.ds(BELOW, 4)], window.at[pl.ds(2, 4)], 1, r),
        push(window.at[pl.ds(BELOW, 4)], window.at[pl.ds(10, 4)], -1, r),
    ]

    get_counts.wait()
    filled = c_s[0]
    lowest = d * FRAMES - BELOW
    used = [j < filled for j in range(CAP)]
    none = jnp.zeros((W, C), BF16)

    for box in (inc, act_one, grad_mid, act_two):
        for s in (OWN, NEAR, FAR):
            box[s, 0] = none
            box[s, CAP + 1] = none
    get_raw.wait()
    for j in range(CAP):
        inc[OWN, 1 + j] = jnp.where(used[j], raw[j], none)

    end = jnp.clip(filled - 1, 0, CAP - 1)
    last[0] = raw[end]
    inc_slots = send_slots(inc)
    edges = (
        push(last.at[0], inc_edge.at[0, OWN], 1, r),
        push(inc.at[OWN, 1], inc_edge.at[1, OWN], -1, r),
    )
    inc_edges = [edges]
    get_frames.wait()
    get_weights.wait()
    def products(fields, w, s, back, c, depths):
        tap = (1, near_tap, far_tap)[s]
        if back:
            tile = jnp.concatenate([w[2 - a, 2 - tap, 2 - c] for a in depths], axis=1)
            dims = (((1,), (1,)), ((), ()))
        else:
            tile = jnp.concatenate([w[a, tap, c] for a in depths], axis=0)
            dims = (((1,), (0,)), ((), ()))
        return lax.dot_general(fields, tile, dims, preferred_element_type=F32)

    def inner(slots, box, w, back, s):
        def step():
            if s != OWN:
                slots[s][0].wait_recv()
            fields = jnp.concatenate(
                [box[s, a : a + CAP].reshape(CAP * W, C) for a in range(3)], axis=1
            )
            for c in range(3):
                term = products(fields, w, s, back, c, (0, 1, 2))
                if s == OWN:
                    parts[c] = term.reshape(CAP, W, C)
                else:
                    parts[c] += term.reshape(CAP, W, C)

        when(far_there if s == FAR else None, step)
        if s != OWN:
            slots[s][4] = False

    def border(edges, edge, w, back, s):
        landed(*edges[s])
        there = far_there if s == FAR else None
        first_edge = jnp.where(both(exists(-1), there), edge[0, s], none)
        after_edge = jnp.where(both(exists(1), there), edge[1, s], none)
        for c in range(3):
            parts[c, 0] += products(first_edge, w, s, back, c, (0,))
            term = products(after_edge, w, s, back, c, (2,))
            if s == OWN:
                after[c] = term
            else:
                after[c] += term

    column = lax.broadcasted_iota(jnp.int32, (W, C), 0)

    def shifted(lower, centre, upper):
        lower = jnp.where(column == 0, 0.0, pltpu.roll(lower, 1, 0))
        upper = jnp.where(column == W - 1, 0.0, pltpu.roll(upper, W - 1, 0))
        return lower + centre + upper

    def slot(j):
        return shifted(parts[0, j], parts[1, j], parts[2, j])

    def joined(extra, j):
        return slot(j) + jnp.where(filled == j + 1, extra, 0.0)

    def inners(slots, box, w, back):
        for s in (OWN, NEAR, FAR):
            inner(slots, box, w, back, s)

    def borders(edges, edge, w, back):
        for s in (OWN, NEAR, FAR):
            border(edges, edge, w, back, s)
        return shifted(after[0], after[1], after[2])

    def convolve(slots, edges, box, edge, w, back):
        inners(slots, box, w, back)
        return borders(edges, edge, w, back)

    get_two.wait()
    inner(inc_slots, inc, w_two, True, OWN)
    inner(inc_slots, inc, w_two, True, NEAR)
    landed(*edges)
    for s, row in ((NEAR, near), (FAR, far)):
        inc_edges.append(
            [
                push(inc_edge.at[k, OWN], inc_edge.at[k, s], 0, row, exists((-1, 1)[k]))
                for k in range(2)
            ]
        )
    inner(inc_slots, inc, w_two, True, FAR)
    landed(*sources)

    def blend(j):
        summed = jnp.zeros((W, C), F32)
        for k in range(TAPS):
            at = jnp.clip(f_s[k, j] - lowest, 0, WINDOW - 1)
            summed += w_s[k, j] * window[at].astype(F32)
        return summed.astype(BF16)

    def silu(value):
        wide = value.astype(F32)
        return (wide * jax.nn.sigmoid(wide)).astype(BF16)

    value = blend(0)
    blended[0] = value
    act_one[OWN, 1] = silu(value)
    last[1] = silu(blend(end))
    act_one_edges = send_edges(act_one, act_one_edge, last.at[1])
    for j in range(1, CAP):
        value = jnp.where(used[j], blend(j), none)
        blended[j] = value
        act_one[OWN, 1 + j] = silu(value)
    act_one_slots = send_slots(act_one)

    extra = borders(inc_edges, inc_edge, w_two, True)
    for j in range(CAP):
        back_two[j] = joined(extra, j)

    get_one.wait()
    get_b_one.wait()
    get_b_two.wait()
    extra = convolve(act_one_slots, act_one_edges, act_one, act_one_edge, w_one, False)

    def first_at(j, conv):
        return (conv + blended[j].astype(F32) + b_one[...]).astype(BF16)

    def grad_at(j, value):
        wide = value.astype(F32)
        gate = jax.nn.sigmoid(wide)
        slope = gate * (1.0 + wide * (1.0 - gate))
        return (raw[j].astype(F32) + slope * back_two[j]).astype(BF16)

    value = first_at(0, joined(extra, 0))
    first[0] = value
    grad_mid[OWN, 1] = grad_at(0, value)
    value = first_at(end, slot(end) + extra)
    last[2] = grad_at(end, value)
    grad_mid_edges = send_edges(grad_mid, grad_mid_edge, last.at[2])
    last[3] = silu(value)
    for j in range(1, CAP):
        value = jnp.where(used[j], first_at(j, joined(extra, j)), none)
        first[j] = value
        grad_mid[OWN, 1 + j] = jnp.where(used[j], grad_at(j, value), none)
    grad_mid_slots = send_slots(grad_mid)
    for j in range(CAP):
        act_two[OWN, 1 + j] = silu(first[j])
    act_two_edges = send_edges(act_two, act_two_edge, last.at[3])
    act_two_slots = send_slots(act_two)
    for j in range(CAP):
        wide = blended[j].astype(F32)
        gate = jax.nn.sigmoid(wide)
        slope_one[j] = gate * (1.0 + wide * (1.0 - gate))
        for f in range(WINDOW):
            weight = jnp.float32(0.0)
            for k in range(TAPS):
                weight += jnp.where(f_s[k, j] == lowest + f, w_s[k, j], 0.0)
            mix[j, f] = jnp.where(used[j], weight, 0.0)

    extra = convolve(grad_mid_slots, grad_mid_edges, grad_mid, grad_mid_edge, w_one, True)
    for j in range(CAP):
        low[j] = grad_mid[OWN, 1 + j].astype(F32) + slope_one[j] * joined(extra, j)

    def gathered(f):
        summed = mix[0, f] * low[0]
        for j in range(1, CAP):
            summed += mix[j, f] * low[j]
        return summed

    spread_copies = []
    for start, count, at, by in ((0, 2, 8, -2), (14, 2, 10, 2), (2, 4, 0, -1), (10, 4, 4, 1)):
        for f in range(start, start + count):
            spread[f] = gathered(f).astype(BF16)
        spread_copies.append(push(spread.at[pl.ds(start, count)], arrived.at[pl.ds(at, count)], by, r))
    for f in range(FRAMES):
        source_grad[f] = gathered(BELOW + f)

    extra = convolve(act_two_slots, act_two_edges, act_two, act_two_edge, w_two, False)
    for j in range(CAP):
        value = joined(extra, j) + first[j].astype(F32) + b_two[...]
        decoded[j] = jnp.where(used[j], value, 0.0).astype(BF16)

    landed(*spread_copies)
    for f in range(FRAMES):
        value = source_grad[f]
        value += jnp.where(exists(1), arrived[f].astype(F32), 0.0)
        value += jnp.where(exists(-1), arrived[4 + f].astype(F32), 0.0)
        if f >= 2:
            value += jnp.where(exists(2), arrived[8 + f - 2].astype(F32), 0.0)
        else:
            value += jnp.where(exists(-2), arrived[10 + f].astype(F32), 0.0)
        source_grad[f] = value
    left(*copies)


def finish(decoded_in, grad_in, decoded, source_grad, done):
    one = pltpu.make_async_copy(decoded_in, decoded, done.at[0])
    two = pltpu.make_async_copy(grad_in, source_grad, done.at[1])
    one.start()
    two.start()
    one.wait()
    two.wait()


def solution(mesh):
    spans, lines = mesh.shape["tm"], mesh.shape["rows"]

    def body(
        source,
        frame_counts,
        tap_frames,
        tap_weights,
        kernel_one,
        bias_one,
        kernel_two,
        bias_two,
        upstream,
    ):
        box = pltpu.VMEM((3, CAP + 2, W, C), BF16)
        edge = pltpu.VMEM((2, 3, W, C), BF16)
        slots = pltpu.VMEM((CAP, W, C), BF16)
        wide_slots = pltpu.VMEM((CAP, W, C), F32)
        kernels = pltpu.VMEM((3, 3, 3, C, C), BF16)
        bias = pltpu.VMEM((1, C), F32)
        decoded, source_grad = pl.pallas_call(
            lambda *refs: kernel(spans, lines, *refs),
            out_shape=(
                pltpu.VMEM((CAP, W, C), BF16),
                pltpu.VMEM((FRAMES, W, C), F32),
            ),
            in_specs=[pl.BlockSpec(memory_space=pl.ANY)] * 9,
            out_specs=[pl.BlockSpec(memory_space=pltpu.VMEM)] * 2,
            scratch_shapes=[
                pltpu.VMEM((WINDOW, W, C), BF16),
                kernels,
                kernels,
                bias,
                bias,
                slots,
                slots,
                slots,
                wide_slots,
                wide_slots,
                wide_slots,
                pltpu.VMEM((3, CAP, W, C), F32),
                pltpu.VMEM((3, W, C), F32),
                box,
                box,
                box,
                box,
                edge,
                edge,
                edge,
                edge,
                pltpu.VMEM((4, W, C), BF16),
                pltpu.VMEM((WINDOW, W, C), BF16),
                pltpu.VMEM((12, W, C), BF16),
                pltpu.SMEM((CAP, WINDOW), F32),
                pltpu.SMEM((1,), jnp.int32),
                pltpu.SMEM((TAPS, CAP), jnp.int32),
                pltpu.SMEM((TAPS, CAP), F32),
                pltpu.SemaphoreType.DMA((9,)),
                pltpu.SemaphoreType.DMA((40,)),
                pltpu.SemaphoreType.DMA((40,)),
            ],
            compiler_params=pltpu.CompilerParams(
                collective_id=0, has_side_effects=True, vmem_limit_bytes=48 * 1024 * 1024
            ),
            cost_estimate=pl.CostEstimate(
                flops=4 * 2 * CAP * W * 27 * C * C,
                bytes_accessed=2 * 27 * C * C * 2,
                transcendentals=0,
            ),
        )(
            *(
                x if x is frame_counts else pltpu.with_memory_space_constraint(x, pltpu.HBM)
                for x in (
                    source.reshape(FRAMES, W, C),
                    frame_counts,
                    tap_frames.T,
                    tap_weights.T,
                    kernel_one,
                    bias_one.reshape(1, C),
                    kernel_two,
                    bias_two.reshape(1, C),
                    upstream.reshape(CAP, W, C),
                )
            )
        )
        decoded, source_grad = pl.pallas_call(
            finish,
            out_shape=(
                jax.ShapeDtypeStruct((CAP, W, C), BF16),
                jax.ShapeDtypeStruct((FRAMES, W, C), F32),
            ),
            in_specs=[pl.BlockSpec(memory_space=pltpu.VMEM)] * 2,
            out_specs=[pl.BlockSpec(memory_space=pl.ANY)] * 2,
            scratch_shapes=[pltpu.SemaphoreType.DMA((2,))],
        )(*(pltpu.with_memory_space_constraint(x, pltpu.VMEM) for x in (decoded, source_grad)))
        return decoded.reshape(CAP, 1, W, C), source_grad.reshape(FRAMES, 1, W, C)

    whole = P("tm", "rows", None, None)
    return jax.shard_map(
        body,
        mesh=mesh,
        in_specs=(whole, P("tm"), P("tm", None), P("tm", None), P(), P(), P(), P(), whole),
        out_specs=(whole, whole),
        check_vma=False,
    )
```

```python
import jax
import jax.numpy as jnp
from jax import lax
from jax.experimental import pallas as pl
from jax.experimental.pallas import tpu as pltpu
from jax.sharding import PartitionSpec as P

MESH = pl.DeviceIdType.MESH
FRAMES = 4
CAP = 9
TAPS = 4
WINDOW = 16
BELOW = 6
W = 32
C = 256
OWN, NEAR, FAR = 0, 1, 2
BF16 = jnp.bfloat16
F32 = jnp.float32


def kernel(
    spans,
    lines,
    source,
    counts,
    frames,
    weights,
    kernel_one,
    bias_one,
    kernel_two,
    bias_two,
    upstream,
    decoded,
    source_grad,
    window,
    w_one,
    w_two,
    b_one,
    b_two,
    raw,
    blended,
    first,
    low,
    back_two,
    slope_one,
    parts,
    fringe,
    plain,
    partial,
    inc,
    act_one,
    grad_mid,
    act_two,
    inc_edge,
    act_one_edge,
    grad_mid_edge,
    act_two_edge,
    last,
    spread,
    arrived,
    mix,
    c_s,
    f_s,
    w_s,
    local,
    send,
    recv,
):
    d = lax.axis_index("tm")
    r = lax.axis_index("rows")
    odd = lax.rem(r, 2)
    near = r + 1 - 2 * odd
    far = lax.rem(r - 1 + 2 * odd + lines, lines)
    far_there = jnp.where(odd == 0, r > 0, r < lines - 1)
    near_tap = 2 - 2 * odd
    far_tap = 2 * odd

    upper = spans - 1

    def exists(by):
        if by == 0:
            return None
        return d >= -by if by < 0 else d <= upper - by

    def both(one, two):
        if one is None or two is None:
            return two if one is None else one
        return one & two

    def when(condition, action):
        if condition is None:
            action()
        else:
            pl.when(condition)(action)

    def line(row):
        return far_there if row is far else None

    reach = [(by, r) for by in (-2, -1, 1, 2)] + [(0, near), (0, far)]
    barrier = pltpu.get_barrier_semaphore()
    greeted = jnp.int32(0)
    for by, row in reach:
        there = both(exists(by), line(row))

        def greet(by=by, row=row):
            pl.semaphore_signal(
                barrier, inc=1, device_id={"tm": d + by, "rows": row}, device_id_type=MESH
            )

        when(there, greet)
        greeted += 1 if there is None else jnp.where(there, 1, 0)

    def fetch(k, src, dst):
        copy = pltpu.make_async_copy(src, dst, local.at[k])
        copy.start()
        fetched.append(copy)
        return copy

    fetched = []
    get_source = fetch(0, source, window.at[pl.ds(BELOW, FRAMES)])
    get_raw = fetch(4, upstream, raw)
    get_counts = fetch(1, counts, c_s)
    get_frames = fetch(2, frames, f_s)
    get_weights = fetch(3, weights, w_s)
    get_two = fetch(5, kernel_two, w_two)
    get_one = fetch(6, kernel_one, w_one)
    get_b_one = fetch(7, bias_one, b_one)
    get_b_two = fetch(8, bias_two, b_two)

    copies = []

    def push(src, dst, by, row, held=None):
        k = len(copies)
        copy = pltpu.make_async_remote_copy(
            src_ref=src,
            dst_ref=dst,
            send_sem=send.at[k],
            recv_sem=recv.at[k],
            device_id={"tm": d + by, "rows": row},
            device_id_type=MESH,
        )
        sent = both(both(exists(by), line(row)), held)
        when(sent, copy.start)
        entry = [copy, sent, both(both(exists(-by), line(row)), held), True, True]
        copies.append(entry)
        return entry

    def landed(*entries):
        for entry in entries:
            if entry[4]:
                when(entry[2], entry[0].wait_recv)
                entry[4] = False

    def left(*entries):
        for entry in entries:
            if entry[3]:
                when(entry[1], entry[0].wait_send)
                entry[3] = False

    def send_edges(box, edge, ends):
        head = box.at[OWN, 1]
        far_edges = push(ends, edge.at[0, FAR], 1, far), push(head, edge.at[1, FAR], -1, far)
        own_edges = push(ends, edge.at[0, OWN], 1, r), push(head, edge.at[1, OWN], -1, r)
        near_edges = push(ends, edge.at[0, NEAR], 1, near), push(head, edge.at[1, NEAR], -1, near)
        return own_edges, near_edges, far_edges

    def send_slots(box):
        mine = box.at[OWN, pl.ds(1, CAP)]
        far_mine = push(mine, box.at[FAR, pl.ds(1, CAP)], 0, far)
        near_mine = push(mine, box.at[NEAR, pl.ds(1, CAP)], 0, near)
        return None, near_mine, far_mine

    get_source.wait()
    pl.semaphore_wait(barrier, greeted)
    sources = [
        push(window.at[pl.ds(BELOW + 2, 2)], window.at[pl.ds(0, 2)], 2, r),
        push(window.at[pl.ds(BELOW, 2)], window.at[pl.ds(14, 2)], -2, r),
        push(window.at[pl.ds(BELOW, 4)], window.at[pl.ds(2, 4)], 1, r),
        push(window.at[pl.ds(BELOW, 4)], window.at[pl.ds(10, 4)], -1, r),
    ]

    get_counts.wait()
    filled = c_s[0]
    lowest = d * FRAMES - BELOW
    used = [j < filled for j in range(CAP)]
    none = jnp.zeros((W, C), BF16)

    for box in (inc, act_one, grad_mid, act_two):
        for s in (OWN, NEAR, FAR):
            box[s, 0] = none
            box[s, CAP + 1] = none
    get_raw.wait()
    for j in range(CAP):
        inc[OWN, 1 + j] = jnp.where(used[j], raw[j], none)

    end = jnp.clip(filled - 1, 0, CAP - 1)
    last[0] = raw[end]
    inc_slots = send_slots(inc)
    edges = (
        push(last.at[0], inc_edge.at[0, OWN], 1, r),
        push(inc.at[OWN, 1], inc_edge.at[1, OWN], -1, r),
    )
    inc_edges = [edges]
    get_frames.wait()
    get_weights.wait()
    def products(fields, w, s, back, c, depths):
        tap = (1, near_tap, far_tap)[s]
        if back:
            tile = jnp.concatenate([w[2 - a, 2 - tap, 2 - c] for a in depths], axis=1)
            dims = (((1,), (1,)), ((), ()))
        else:
            tile = jnp.concatenate([w[a, tap, c] for a in depths], axis=0)
            dims = (((1,), (0,)), ((), ()))
        return lax.dot_general(fields, tile, dims, preferred_element_type=F32)

    def inner(slots, box, w, back, s):
        def step():
            if s != OWN:
                slots[s][0].wait_recv()
            fields = jnp.concatenate(
                [box[s, a : a + CAP].reshape(CAP * W, C) for a in range(3)], axis=1
            )
            for c in range(3):
                term = products(fields, w, s, back, c, (0, 1, 2))
                if s == OWN:
                    parts[c] = term.reshape(CAP, W, C)
                else:
                    parts[c] += term.reshape(CAP, W, C)

        when(far_there if s == FAR else None, step)
        if s != OWN:
            slots[s][4] = False

    def border(edges, edge, w, back, s):
        landed(*edges[s])
        there = far_there if s == FAR else None
        first_edge = jnp.where(both(exists(-1), there), edge[0, s], none)
        after_edge = jnp.where(both(exists(1), there), edge[1, s], none)
        for c in range(3):
            for side, field, depth in ((0, first_edge, 0), (1, after_edge, 2)):
                term = products(field, w, s, back, c, (depth,))
                if s == OWN:
                    fringe[side, c] = term
                else:
                    fringe[side, c] += term

    column = lax.broadcasted_iota(jnp.int32, (W, C), 0)

    def shifted(lower, centre, upper):
        lower = jnp.where(column == 0, 0.0, pltpu.roll(lower, 1, 0))
        upper = jnp.where(column == W - 1, 0.0, pltpu.roll(upper, W - 1, 0))
        return lower + centre + upper

    def slot(j):
        return shifted(parts[0, j], parts[1, j], parts[2, j])

    def inners(slots, box, w, back):
        for s in (OWN, NEAR, FAR):
            inner(slots, box, w, back, s)

    def borders(edges, edge, w, back):
        for s in (OWN, NEAR, FAR):
            border(edges, edge, w, back, s)
        return (shifted(*(fringe[side, c] for c in range(3))) for side in range(2))

    def patched(value, j, start, stop):
        if j == 0:
            value = value + start
        return value + jnp.where(filled == j + 1, stop, 0.0)

    for j in range(CAP):
        tap_at = [f_s[k, j] - lowest for k in range(TAPS)]
        tap_by = [jnp.where(used[j], w_s[k, j], 0.0) for k in range(TAPS)]
        for f in range(WINDOW):
            weight = jnp.float32(0.0)
            for k in range(TAPS):
                weight += jnp.where(tap_at[k] == f, tap_by[k], 0.0)
            mix[j, f] = weight

    get_two.wait()
    inner(inc_slots, inc, w_two, True, OWN)
    inner(inc_slots, inc, w_two, True, NEAR)
    landed(*edges)
    for s, row in ((NEAR, near), (FAR, far)):
        inc_edges.append(
            [
                push(inc_edge.at[k, OWN], inc_edge.at[k, s], 0, row, exists((-1, 1)[k]))
                for k in range(2)
            ]
        )
    inner(inc_slots, inc, w_two, True, FAR)
    for j in range(CAP):
        back_two[j] = slot(j)
    landed(*sources)

    def blend(j):
        summed = jnp.zeros((W, C), F32)
        for k in range(TAPS):
            at = jnp.clip(f_s[k, j] - lowest, 0, WINDOW - 1)
            summed += w_s[k, j] * window[at].astype(F32)
        return summed.astype(BF16)

    def silu(value):
        wide = value.astype(F32)
        return (wide * jax.nn.sigmoid(wide)).astype(BF16)

    value = blend(0)
    blended[0] = value
    act_one[OWN, 1] = silu(value)
    last[1] = silu(blend(end))
    act_one_edges = send_edges(act_one, act_one_edge, last.at[1])
    for j in range(1, CAP):
        value = jnp.where(used[j], blend(j), none)
        blended[j] = value
        act_one[OWN, 1 + j] = silu(value)
    act_one_slots = send_slots(act_one)

    start, stop = borders(inc_edges, inc_edge, w_two, True)
    for j in range(CAP):
        back_two[j] = patched(back_two[j], j, start, stop)

    def slope(value):
        wide = value.astype(F32)
        gate = jax.nn.sigmoid(wide)
        return gate * (1.0 + wide * (1.0 - gate))

    for j in range(CAP):
        slope_one[j] = slope(blended[j])

    def grad_at(j, value):
        return (raw[j].astype(F32) + slope(value) * back_two[j]).astype(BF16)

    get_one.wait()
    get_b_one.wait()
    get_b_two.wait()
    inners(act_one_slots, act_one, w_one, False)
    for j in range(CAP):
        value = slot(j) + blended[j].astype(F32) + b_one[...]
        plain[j] = value
        if j > 0:
            value = jnp.where(used[j], value.astype(BF16), none)
            first[j] = value
            grad_mid[OWN, 1 + j] = jnp.where(used[j], grad_at(j, value), none)
            act_two[OWN, 1 + j] = silu(value)
    start, stop = borders(act_one_edges, act_one_edge, w_one, False)
    value = patched(plain[0], 0, start, stop).astype(BF16)
    first[0] = value
    grad_mid[OWN, 1] = grad_at(0, value)
    stop_first = (plain[end] + stop + jnp.where(end == 0, start, 0.0)).astype(BF16)
    stop_grad = grad_at(end, stop_first)
    last[2] = stop_grad
    grad_mid_edges = send_edges(grad_mid, grad_mid_edge, last.at[2])
    for j in range(1, CAP):
        at_end = filled == j + 1
        grad_mid[OWN, 1 + j] = jnp.where(at_end, stop_grad, grad_mid[OWN, 1 + j])
    grad_mid_slots = send_slots(grad_mid)
    act_two[OWN, 1] = silu(value)
    stop_act = silu(stop_first)
    last[3] = stop_act
    for j in range(1, CAP):
        at_end = filled == j + 1
        first[j] = jnp.where(at_end, stop_first, first[j])
        act_two[OWN, 1 + j] = jnp.where(at_end, stop_act, act_two[OWN, 1 + j])
    act_two_edges = send_edges(act_two, act_two_edge, last.at[3])
    act_two_slots = send_slots(act_two)

    inners(grad_mid_slots, grad_mid, w_one, True)
    for j in range(CAP):
        low[j] = grad_mid[OWN, 1 + j].astype(F32) + slope_one[j] * slot(j)
    for f in range(WINDOW):
        summed = mix[0, f] * low[0]
        for j in range(1, CAP):
            summed += mix[j, f] * low[j]
        partial[f] = summed
    start, stop = borders(grad_mid_edges, grad_mid_edge, w_one, True)
    start = slope_one[0] * start
    stop = slope_one[end] * stop

    def gathered(f):
        return partial[f] + mix[0, f] * start + mix[end, f] * stop

    spread_copies = []
    for head, count, at, by in ((0, 2, 8, -2), (14, 2, 10, 2), (2, 4, 0, -1), (10, 4, 4, 1)):
        for f in range(head, head + count):
            spread[f] = gathered(f).astype(BF16)
        spread_copies.append(push(spread.at[pl.ds(head, count)], arrived.at[pl.ds(at, count)], by, r))
    for f in range(FRAMES):
        source_grad[f] = gathered(BELOW + f)

    inners(act_two_slots, act_two, w_two, False)
    start, stop = borders(act_two_edges, act_two_edge, w_two, False)
    for j in range(CAP):
        value = patched(slot(j), j, start, stop) + first[j].astype(F32) + b_two[...]
        decoded[j] = jnp.where(used[j], value, 0.0).astype(BF16)

    landed(*spread_copies)
    for f in range(FRAMES):
        value = source_grad[f]
        value += jnp.where(exists(1), arrived[f].astype(F32), 0.0)
        value += jnp.where(exists(-1), arrived[4 + f].astype(F32), 0.0)
        if f >= 2:
            value += jnp.where(exists(2), arrived[8 + f - 2].astype(F32), 0.0)
        else:
            value += jnp.where(exists(-2), arrived[10 + f].astype(F32), 0.0)
        source_grad[f] = value
    left(*copies)


def finish(decoded_in, grad_in, decoded, source_grad, done):
    one = pltpu.make_async_copy(decoded_in, decoded, done.at[0])
    two = pltpu.make_async_copy(grad_in, source_grad, done.at[1])
    one.start()
    two.start()
    one.wait()
    two.wait()


def solution(mesh):
    spans, lines = mesh.shape["tm"], mesh.shape["rows"]

    def body(
        source,
        frame_counts,
        tap_frames,
        tap_weights,
        kernel_one,
        bias_one,
        kernel_two,
        bias_two,
        upstream,
    ):
        box = pltpu.VMEM((3, CAP + 2, W, C), BF16)
        edge = pltpu.VMEM((2, 3, W, C), BF16)
        slots = pltpu.VMEM((CAP, W, C), BF16)
        wide_slots = pltpu.VMEM((CAP, W, C), F32)
        kernels = pltpu.VMEM((3, 3, 3, C, C), BF16)
        bias = pltpu.VMEM((1, C), F32)
        decoded, source_grad = pl.pallas_call(
            lambda *refs: kernel(spans, lines, *refs),
            out_shape=(
                pltpu.VMEM((CAP, W, C), BF16),
                pltpu.VMEM((FRAMES, W, C), F32),
            ),
            in_specs=[pl.BlockSpec(memory_space=pl.ANY)] * 9,
            out_specs=[pl.BlockSpec(memory_space=pltpu.VMEM)] * 2,
            scratch_shapes=[
                pltpu.VMEM((WINDOW, W, C), BF16),
                kernels,
                kernels,
                bias,
                bias,
                slots,
                slots,
                slots,
                wide_slots,
                wide_slots,
                wide_slots,
                pltpu.VMEM((3, CAP, W, C), F32),
                pltpu.VMEM((2, 3, W, C), F32),
                wide_slots,
                pltpu.VMEM((WINDOW, W, C), F32),
                box,
                box,
                box,
                box,
                edge,
                edge,
                edge,
                edge,
                pltpu.VMEM((4, W, C), BF16),
                pltpu.VMEM((WINDOW, W, C), BF16),
                pltpu.VMEM((12, W, C), BF16),
                pltpu.SMEM((CAP, WINDOW), F32),
                pltpu.SMEM((1,), jnp.int32),
                pltpu.SMEM((TAPS, CAP), jnp.int32),
                pltpu.SMEM((TAPS, CAP), F32),
                pltpu.SemaphoreType.DMA((9,)),
                pltpu.SemaphoreType.DMA((40,)),
                pltpu.SemaphoreType.DMA((40,)),
            ],
            compiler_params=pltpu.CompilerParams(
                collective_id=0, has_side_effects=True, vmem_limit_bytes=48 * 1024 * 1024
            ),
            cost_estimate=pl.CostEstimate(
                flops=4 * 2 * CAP * W * 27 * C * C,
                bytes_accessed=2 * 27 * C * C * 2,
                transcendentals=0,
            ),
        )(
            *(
                x if x is frame_counts else pltpu.with_memory_space_constraint(x, pltpu.HBM)
                for x in (
                    source.reshape(FRAMES, W, C),
                    frame_counts,
                    tap_frames.T,
                    tap_weights.T,
                    kernel_one,
                    bias_one.reshape(1, C),
                    kernel_two,
                    bias_two.reshape(1, C),
                    upstream.reshape(CAP, W, C),
                )
            )
        )
        decoded, source_grad = pl.pallas_call(
            finish,
            out_shape=(
                jax.ShapeDtypeStruct((CAP, W, C), BF16),
                jax.ShapeDtypeStruct((FRAMES, W, C), F32),
            ),
            in_specs=[pl.BlockSpec(memory_space=pltpu.VMEM)] * 2,
            out_specs=[pl.BlockSpec(memory_space=pl.ANY)] * 2,
            scratch_shapes=[pltpu.SemaphoreType.DMA((2,))],
        )(*(pltpu.with_memory_space_constraint(x, pltpu.VMEM) for x in (decoded, source_grad)))
        return decoded.reshape(CAP, 1, W, C), source_grad.reshape(FRAMES, 1, W, C)

    whole = P("tm", "rows", None, None)
    return jax.shard_map(
        body,
        mesh=mesh,
        in_specs=(whole, P("tm"), P("tm", None), P("tm", None), P(), P(), P(), P(), whole),
        out_specs=(whole, whole),
        check_vma=False,
    )
```

```python
import jax
import jax.numpy as jnp
from jax import lax
from jax.experimental import pallas as pl
from jax.experimental.pallas import tpu as pltpu
from jax.sharding import PartitionSpec as P

MESH = pl.DeviceIdType.MESH
FRAMES = 4
CAP = 9
TAPS = 4
WINDOW = 16
BELOW = 6
W = 32
C = 256
OWN, NEAR, FAR = 0, 1, 2
ENDS = {3: (0, 4), 6: (4, 7), 8: (7, 9)}
BF16 = jnp.bfloat16
F32 = jnp.float32


def kernel(
    spans,
    lines,
    source,
    counts,
    frames,
    weights,
    kernel_one,
    bias_one,
    kernel_two,
    bias_two,
    upstream,
    decoded,
    source_grad,
    window,
    w_one,
    w_two,
    b_one,
    b_two,
    raw,
    blended,
    first,
    low,
    back_two,
    slope_one,
    parts,
    fringe,
    plain,
    partial,
    inc,
    act_one,
    grad_mid,
    act_two,
    inc_edge,
    act_one_edge,
    grad_mid_edge,
    act_two_edge,
    last,
    spread,
    arrived,
    mix,
    c_s,
    f_s,
    w_s,
    local,
    send,
    recv,
):
    d = lax.axis_index("tm")
    r = lax.axis_index("rows")
    odd = lax.rem(r, 2)
    near = r + 1 - 2 * odd
    far = lax.rem(r - 1 + 2 * odd + lines, lines)
    far_there = jnp.where(odd == 0, r > 0, r < lines - 1)
    near_tap = 2 - 2 * odd
    far_tap = 2 * odd

    upper = spans - 1

    def exists(by):
        if by == 0:
            return None
        return d >= -by if by < 0 else d <= upper - by

    def both(one, two):
        if one is None or two is None:
            return two if one is None else one
        return one & two

    def when(condition, action):
        if condition is None:
            action()
        else:
            pl.when(condition)(action)

    def line(row):
        return far_there if row is far else None

    reach = [(by, r) for by in (-2, -1, 1, 2)] + [(0, near), (0, far)]
    barrier = pltpu.get_barrier_semaphore()
    greeted = jnp.int32(0)
    for by, row in reach:
        there = both(exists(by), line(row))

        def greet(by=by, row=row):
            pl.semaphore_signal(
                barrier, inc=1, device_id={"tm": d + by, "rows": row}, device_id_type=MESH
            )

        when(there, greet)
        greeted += 1 if there is None else jnp.where(there, 1, 0)

    def fetch(k, src, dst):
        copy = pltpu.make_async_copy(src, dst, local.at[k])
        copy.start()
        fetched.append(copy)
        return copy

    fetched = []
    get_source = fetch(0, source, window.at[pl.ds(BELOW, FRAMES)])
    get_raw = fetch(4, upstream, raw)
    get_counts = fetch(1, counts, c_s)
    get_frames = fetch(2, frames, f_s)
    get_weights = fetch(3, weights, w_s)
    get_two = fetch(5, kernel_two, w_two)
    get_one = fetch(6, kernel_one, w_one)
    get_b_one = fetch(7, bias_one, b_one)
    get_b_two = fetch(8, bias_two, b_two)

    copies = []

    def push(src, dst, by, row, held=None):
        k = len(copies)
        copy = pltpu.make_async_remote_copy(
            src_ref=src,
            dst_ref=dst,
            send_sem=send.at[k],
            recv_sem=recv.at[k],
            device_id={"tm": d + by, "rows": row},
            device_id_type=MESH,
        )
        sent = both(both(exists(by), line(row)), held)
        when(sent, copy.start)
        entry = [copy, sent, both(both(exists(-by), line(row)), held), True, True]
        copies.append(entry)
        return entry

    def landed(*entries):
        for entry in entries:
            if entry[4]:
                when(entry[2], entry[0].wait_recv)
                entry[4] = False

    def left(*entries):
        for entry in entries:
            if entry[3]:
                when(entry[1], entry[0].wait_send)
                entry[3] = False

    def send_edges(box, edge, ends):
        head = box.at[OWN, 1]
        far_edges = push(ends, edge.at[0, FAR], 1, far), push(head, edge.at[1, FAR], -1, far)
        own_edges = push(ends, edge.at[0, OWN], 1, r), push(head, edge.at[1, OWN], -1, r)
        near_edges = push(ends, edge.at[0, NEAR], 1, near), push(head, edge.at[1, NEAR], -1, near)
        return own_edges, near_edges, far_edges

    def send_far(box, low_slot, high_slot):
        span = pl.ds(1 + low_slot, high_slot - low_slot)
        return push(box.at[OWN, span], box.at[FAR, span], 0, far)

    def send_near(box):
        span = pl.ds(1, CAP)
        return push(box.at[OWN, span], box.at[NEAR, span], 0, near)

    get_source.wait()
    pl.semaphore_wait(barrier, greeted)
    sources = [
        push(window.at[pl.ds(BELOW + 2, 2)], window.at[pl.ds(0, 2)], 2, r),
        push(window.at[pl.ds(BELOW, 2)], window.at[pl.ds(14, 2)], -2, r),
        push(window.at[pl.ds(BELOW, 4)], window.at[pl.ds(2, 4)], 1, r),
        push(window.at[pl.ds(BELOW, 4)], window.at[pl.ds(10, 4)], -1, r),
    ]

    get_counts.wait()
    filled = c_s[0]
    lowest = d * FRAMES - BELOW
    used = [j < filled for j in range(CAP)]
    none = jnp.zeros((W, C), BF16)

    for box in (inc, act_one, grad_mid, act_two):
        for s in (OWN, NEAR, FAR):
            box[s, 0] = none
            box[s, CAP + 1] = none
    get_raw.wait()
    for j in range(CAP):
        inc[OWN, 1 + j] = jnp.where(used[j], raw[j], none)

    end = jnp.clip(filled - 1, 0, CAP - 1)
    last[0] = raw[end]
    inc_slots = (None, [send_near(inc)], [send_far(inc, 0, CAP)])
    edges = (
        push(last.at[0], inc_edge.at[0, OWN], 1, r),
        push(inc.at[OWN, 1], inc_edge.at[1, OWN], -1, r),
    )
    inc_edges = [edges]
    get_frames.wait()
    get_weights.wait()
    def products(fields, w, s, back, c, depths):
        tap = (1, near_tap, far_tap)[s]
        if back:
            tile = jnp.concatenate([w[2 - a, 2 - tap, 2 - c] for a in depths], axis=1)
            dims = (((1,), (1,)), ((), ()))
        else:
            tile = jnp.concatenate([w[a, tap, c] for a in depths], axis=0)
            dims = (((1,), (0,)), ((), ()))
        return lax.dot_general(fields, tile, dims, preferred_element_type=F32)

    def inner(slots, box, w, back, s):
        def step():
            pieces = 1 if s == OWN else len(slots[s])
            for k in range(pieces):
                if s != OWN:
                    slots[s][k][0].wait_recv()
                low_slot, high_slot = (0, CAP) if pieces == 1 else (3 * k, 3 * k + 3)
                held = high_slot - low_slot
                fields = jnp.concatenate(
                    [
                        box[s, low_slot + a : high_slot + a].reshape(held * W, C)
                        for a in range(3)
                    ],
                    axis=1,
                )
                for c in range(3):
                    term = products(fields, w, s, back, c, (0, 1, 2)).reshape(held, W, C)
                    if s == OWN:
                        parts[c] = term
                    else:
                        parts[c, low_slot:high_slot] += term

        when(far_there if s == FAR else None, step)
        if s != OWN:
            for entry in slots[s]:
                entry[4] = False

    def border(edges, edge, w, back, s):
        landed(*edges[s])
        there = far_there if s == FAR else None
        first_edge = jnp.where(both(exists(-1), there), edge[0, s], none)
        after_edge = jnp.where(both(exists(1), there), edge[1, s], none)
        for c in range(3):
            for side, field, depth in ((0, first_edge, 0), (1, after_edge, 2)):
                term = products(field, w, s, back, c, (depth,))
                if s == OWN:
                    fringe[side, c] = term
                else:
                    fringe[side, c] += term

    column = lax.broadcasted_iota(jnp.int32, (W, C), 0)

    def shifted(lower, centre, upper):
        lower = jnp.where(column == 0, 0.0, pltpu.roll(lower, 1, 0))
        upper = jnp.where(column == W - 1, 0.0, pltpu.roll(upper, W - 1, 0))
        return lower + centre + upper

    def slot(j):
        return shifted(parts[0, j], parts[1, j], parts[2, j])

    def inners(slots, box, w, back):
        for s in (OWN, NEAR, FAR):
            inner(slots, box, w, back, s)

    def borders(edges, edge, w, back):
        for s in (OWN, NEAR, FAR):
            border(edges, edge, w, back, s)
        return (shifted(*(fringe[side, c] for c in range(3))) for side in range(2))

    def patched(value, j, start, stop):
        if j == 0:
            value = value + start
        return value + jnp.where(filled == j + 1, stop, 0.0)

    for j in range(CAP):
        tap_at = [f_s[k, j] - lowest for k in range(TAPS)]
        tap_by = [jnp.where(used[j], w_s[k, j], 0.0) for k in range(TAPS)]
        for f in range(WINDOW):
            weight = jnp.float32(0.0)
            for k in range(TAPS):
                weight += jnp.where(tap_at[k] == f, tap_by[k], 0.0)
            mix[j, f] = weight

    get_two.wait()
    inner(inc_slots, inc, w_two, True, OWN)
    inner(inc_slots, inc, w_two, True, NEAR)
    landed(*edges)
    for s, row in ((NEAR, near), (FAR, far)):
        inc_edges.append(
            [
                push(inc_edge.at[k, OWN], inc_edge.at[k, s], 0, row, exists((-1, 1)[k]))
                for k in range(2)
            ]
        )
    inner(inc_slots, inc, w_two, True, FAR)
    for j in range(CAP):
        back_two[j] = slot(j)
    landed(*sources)

    def blend(j):
        summed = jnp.zeros((W, C), F32)
        for k in range(TAPS):
            at = jnp.clip(f_s[k, j] - lowest, 0, WINDOW - 1)
            summed += w_s[k, j] * window[at].astype(F32)
        return summed.astype(BF16)

    def silu(value):
        wide = value.astype(F32)
        return (wide * jax.nn.sigmoid(wide)).astype(BF16)

    value = blend(0)
    blended[0] = value
    act_one[OWN, 1] = silu(value)
    last[1] = silu(blend(end))
    act_one_edges = send_edges(act_one, act_one_edge, last.at[1])
    act_one_far = []
    for j in range(1, CAP):
        value = jnp.where(used[j], blend(j), none)
        blended[j] = value
        act_one[OWN, 1 + j] = silu(value)
        if j in ENDS:
            act_one_far.append(send_far(act_one, *ENDS[j]))
    act_one_slots = (None, [send_near(act_one)], act_one_far)

    start, stop = borders(inc_edges, inc_edge, w_two, True)
    for j in range(CAP):
        back_two[j] = patched(back_two[j], j, start, stop)

    def slope(value):
        wide = value.astype(F32)
        gate = jax.nn.sigmoid(wide)
        return gate * (1.0 + wide * (1.0 - gate))

    for j in range(CAP):
        slope_one[j] = slope(blended[j])

    def grad_at(j, value):
        return (raw[j].astype(F32) + slope(value) * back_two[j]).astype(BF16)

    get_one.wait()
    get_b_one.wait()
    get_b_two.wait()
    inners(act_one_slots, act_one, w_one, False)
    for j in range(CAP):
        value = slot(j) + blended[j].astype(F32) + b_one[...]
        plain[j] = value
        if j > 0:
            value = jnp.where(used[j], value.astype(BF16), none)
            first[j] = value
            grad_mid[OWN, 1 + j] = jnp.where(used[j], grad_at(j, value), none)
            act_two[OWN, 1 + j] = silu(value)
    start, stop = borders(act_one_edges, act_one_edge, w_one, False)
    value = patched(plain[0], 0, start, stop).astype(BF16)
    first[0] = value
    grad_mid[OWN, 1] = grad_at(0, value)
    stop_first = (plain[end] + stop + jnp.where(end == 0, start, 0.0)).astype(BF16)
    stop_grad = grad_at(end, stop_first)
    last[2] = stop_grad
    grad_mid_edges = send_edges(grad_mid, grad_mid_edge, last.at[2])
    grad_mid_far = []
    for j in range(1, CAP):
        at_end = filled == j + 1
        grad_mid[OWN, 1 + j] = jnp.where(at_end, stop_grad, grad_mid[OWN, 1 + j])
        if j in ENDS:
            grad_mid_far.append(send_far(grad_mid, *ENDS[j]))
    grad_mid_slots = (None, [send_near(grad_mid)], grad_mid_far)
    act_two[OWN, 1] = silu(value)
    stop_act = silu(stop_first)
    last[3] = stop_act
    for j in range(1, CAP):
        at_end = filled == j + 1
        first[j] = jnp.where(at_end, stop_first, first[j])
        act_two[OWN, 1 + j] = jnp.where(at_end, stop_act, act_two[OWN, 1 + j])
    act_two_edges = send_edges(act_two, act_two_edge, last.at[3])
    act_two_slots = (None, [send_near(act_two)], [send_far(act_two, 0, CAP)])

    inners(grad_mid_slots, grad_mid, w_one, True)
    for j in range(CAP):
        low[j] = grad_mid[OWN, 1 + j].astype(F32) + slope_one[j] * slot(j)
    for f in range(WINDOW):
        summed = mix[0, f] * low[0]
        for j in range(1, CAP):
            summed += mix[j, f] * low[j]
        partial[f] = summed
    start, stop = borders(grad_mid_edges, grad_mid_edge, w_one, True)
    start = slope_one[0] * start
    stop = slope_one[end] * stop

    def gathered(f):
        return partial[f] + mix[0, f] * start + mix[end, f] * stop

    spread_copies = []
    for head, count, at, by in ((0, 2, 8, -2), (14, 2, 10, 2), (2, 4, 0, -1), (10, 4, 4, 1)):
        for f in range(head, head + count):
            spread[f] = gathered(f).astype(BF16)
        spread_copies.append(push(spread.at[pl.ds(head, count)], arrived.at[pl.ds(at, count)], by, r))
    for f in range(FRAMES):
        source_grad[f] = gathered(BELOW + f)

    inners(act_two_slots, act_two, w_two, False)
    start, stop = borders(act_two_edges, act_two_edge, w_two, False)
    for j in range(CAP):
        value = patched(slot(j), j, start, stop) + first[j].astype(F32) + b_two[...]
        decoded[j] = jnp.where(used[j], value, 0.0).astype(BF16)

    landed(*spread_copies)
    for f in range(FRAMES):
        value = source_grad[f]
        value += jnp.where(exists(1), arrived[f].astype(F32), 0.0)
        value += jnp.where(exists(-1), arrived[4 + f].astype(F32), 0.0)
        if f >= 2:
            value += jnp.where(exists(2), arrived[8 + f - 2].astype(F32), 0.0)
        else:
            value += jnp.where(exists(-2), arrived[10 + f].astype(F32), 0.0)
        source_grad[f] = value
    left(*copies)


def finish(decoded_in, grad_in, decoded, source_grad, done):
    one = pltpu.make_async_copy(decoded_in, decoded, done.at[0])
    two = pltpu.make_async_copy(grad_in, source_grad, done.at[1])
    one.start()
    two.start()
    one.wait()
    two.wait()


def solution(mesh):
    spans, lines = mesh.shape["tm"], mesh.shape["rows"]

    def body(
        source,
        frame_counts,
        tap_frames,
        tap_weights,
        kernel_one,
        bias_one,
        kernel_two,
        bias_two,
        upstream,
    ):
        box = pltpu.VMEM((3, CAP + 2, W, C), BF16)
        edge = pltpu.VMEM((2, 3, W, C), BF16)
        slots = pltpu.VMEM((CAP, W, C), BF16)
        wide_slots = pltpu.VMEM((CAP, W, C), F32)
        kernels = pltpu.VMEM((3, 3, 3, C, C), BF16)
        bias = pltpu.VMEM((1, C), F32)
        decoded, source_grad = pl.pallas_call(
            lambda *refs: kernel(spans, lines, *refs),
            out_shape=(
                pltpu.VMEM((CAP, W, C), BF16),
                pltpu.VMEM((FRAMES, W, C), F32),
            ),
            in_specs=[pl.BlockSpec(memory_space=pl.ANY)] * 9,
            out_specs=[pl.BlockSpec(memory_space=pltpu.VMEM)] * 2,
            scratch_shapes=[
                pltpu.VMEM((WINDOW, W, C), BF16),
                kernels,
                kernels,
                bias,
                bias,
                slots,
                slots,
                slots,
                wide_slots,
                wide_slots,
                wide_slots,
                pltpu.VMEM((3, CAP, W, C), F32),
                pltpu.VMEM((2, 3, W, C), F32),
                wide_slots,
                pltpu.VMEM((WINDOW, W, C), F32),
                box,
                box,
                box,
                box,
                edge,
                edge,
                edge,
                edge,
                pltpu.VMEM((4, W, C), BF16),
                pltpu.VMEM((WINDOW, W, C), BF16),
                pltpu.VMEM((12, W, C), BF16),
                pltpu.SMEM((CAP, WINDOW), F32),
                pltpu.SMEM((1,), jnp.int32),
                pltpu.SMEM((TAPS, CAP), jnp.int32),
                pltpu.SMEM((TAPS, CAP), F32),
                pltpu.SemaphoreType.DMA((9,)),
                pltpu.SemaphoreType.DMA((44,)),
                pltpu.SemaphoreType.DMA((44,)),
            ],
            compiler_params=pltpu.CompilerParams(
                collective_id=0, has_side_effects=True, vmem_limit_bytes=48 * 1024 * 1024
            ),
            cost_estimate=pl.CostEstimate(
                flops=4 * 2 * CAP * W * 27 * C * C,
                bytes_accessed=2 * 27 * C * C * 2,
                transcendentals=0,
            ),
        )(
            *(
                x if x is frame_counts else pltpu.with_memory_space_constraint(x, pltpu.HBM)
                for x in (
                    source.reshape(FRAMES, W, C),
                    frame_counts,
                    tap_frames.T,
                    tap_weights.T,
                    kernel_one,
                    bias_one.reshape(1, C),
                    kernel_two,
                    bias_two.reshape(1, C),
                    upstream.reshape(CAP, W, C),
                )
            )
        )
        decoded, source_grad = pl.pallas_call(
            finish,
            out_shape=(
                jax.ShapeDtypeStruct((CAP, W, C), BF16),
                jax.ShapeDtypeStruct((FRAMES, W, C), F32),
            ),
            in_specs=[pl.BlockSpec(memory_space=pltpu.VMEM)] * 2,
            out_specs=[pl.BlockSpec(memory_space=pl.ANY)] * 2,
            scratch_shapes=[pltpu.SemaphoreType.DMA((2,))],
        )(*(pltpu.with_memory_space_constraint(x, pltpu.VMEM) for x in (decoded, source_grad)))
        return decoded.reshape(CAP, 1, W, C), source_grad.reshape(FRAMES, 1, W, C)

    whole = P("tm", "rows", None, None)
    return jax.shard_map(
        body,
        mesh=mesh,
        in_specs=(whole, P("tm"), P("tm", None), P("tm", None), P(), P(), P(), P(), whole),
        out_specs=(whole, whole),
        check_vma=False,
    )
```

```python
import jax
import jax.numpy as jnp
from jax import lax
from jax.experimental import pallas as pl
from jax.experimental.pallas import tpu as pltpu
from jax.sharding import PartitionSpec as P

MESH = pl.DeviceIdType.MESH
FRAMES = 4
CAP = 9
TAPS = 4
WINDOW = 16
BELOW = 6
W = 32
C = 256
OWN, NEAR, FAR = 0, 1, 2
BF16 = jnp.bfloat16
F32 = jnp.float32


def kernel(
    spans,
    lines,
    source,
    counts,
    frames,
    weights,
    kernel_one,
    bias_one,
    kernel_two,
    bias_two,
    upstream,
    decoded,
    source_grad,
    window,
    w_one,
    w_two,
    b_one,
    b_two,
    raw,
    blended,
    first,
    low,
    back_two,
    slope_one,
    parts,
    fringe,
    inc,
    act_one,
    grad_mid,
    act_two,
    inc_edge,
    act_one_edge,
    grad_mid_edge,
    act_two_edge,
    last,
    spread,
    arrived,
    mix,
    c_s,
    f_s,
    w_s,
    local,
    send,
    recv,
):
    d = lax.axis_index("tm")
    r = lax.axis_index("rows")
    odd = lax.rem(r, 2)
    near = r + 1 - 2 * odd
    far = lax.rem(r - 1 + 2 * odd + lines, lines)
    far_there = jnp.where(odd == 0, r > 0, r < lines - 1)
    near_tap = 2 - 2 * odd
    far_tap = 2 * odd

    upper = spans - 1

    def exists(by):
        if by == 0:
            return None
        return d >= -by if by < 0 else d <= upper - by

    def both(one, two):
        if one is None or two is None:
            return two if one is None else one
        return one & two

    def when(condition, action):
        if condition is None:
            action()
        else:
            pl.when(condition)(action)

    def line(row):
        return far_there if row is far else None

    reach = [(by, r) for by in (-2, -1, 1, 2)] + [(0, near), (0, far)]
    barrier = pltpu.get_barrier_semaphore()
    greeted = jnp.int32(0)
    for by, row in reach:
        there = both(exists(by), line(row))

        def greet(by=by, row=row):
            pl.semaphore_signal(
                barrier, inc=1, device_id={"tm": d + by, "rows": row}, device_id_type=MESH
            )

        when(there, greet)
        greeted += 1 if there is None else jnp.where(there, 1, 0)

    def fetch(k, src, dst):
        copy = pltpu.make_async_copy(src, dst, local.at[k])
        copy.start()
        fetched.append(copy)
        return copy

    fetched = []
    get_source = fetch(0, source, window.at[pl.ds(BELOW, FRAMES)])
    get_raw = fetch(4, upstream, raw)
    get_counts = fetch(1, counts, c_s)
    get_frames = fetch(2, frames, f_s)
    get_weights = fetch(3, weights, w_s)
    get_two = fetch(5, kernel_two, w_two)
    get_one = fetch(6, kernel_one, w_one)
    get_b_one = fetch(7, bias_one, b_one)
    get_b_two = fetch(8, bias_two, b_two)

    copies = []

    def push(src, dst, by, row, held=None):
        k = len(copies)
        copy = pltpu.make_async_remote_copy(
            src_ref=src,
            dst_ref=dst,
            send_sem=send.at[k],
            recv_sem=recv.at[k],
            device_id={"tm": d + by, "rows": row},
            device_id_type=MESH,
        )
        sent = both(both(exists(by), line(row)), held)
        when(sent, copy.start)
        entry = [copy, sent, both(both(exists(-by), line(row)), held), True, True]
        copies.append(entry)
        return entry

    def landed(*entries):
        for entry in entries:
            if entry[4]:
                when(entry[2], entry[0].wait_recv)
                entry[4] = False

    def left(*entries):
        for entry in entries:
            if entry[3]:
                when(entry[1], entry[0].wait_send)
                entry[3] = False

    def send_edges(box, edge, ends):
        head = box.at[OWN, 1]
        far_edges = push(ends, edge.at[0, FAR], 1, far), push(head, edge.at[1, FAR], -1, far)
        own_edges = push(ends, edge.at[0, OWN], 1, r), push(head, edge.at[1, OWN], -1, r)
        near_edges = push(ends, edge.at[0, NEAR], 1, near), push(head, edge.at[1, NEAR], -1, near)
        return own_edges, near_edges, far_edges

    def send_slots(box):
        mine = box.at[OWN, pl.ds(1, CAP)]
        far_mine = push(mine, box.at[FAR, pl.ds(1, CAP)], 0, far)
        near_mine = push(mine, box.at[NEAR, pl.ds(1, CAP)], 0, near)
        return None, near_mine, far_mine

    get_source.wait()
    pl.semaphore_wait(barrier, greeted)
    sources = [
        push(window.at[pl.ds(BELOW + 2, 2)], window.at[pl.ds(0, 2)], 2, r),
        push(window.at[pl.ds(BELOW, 2)], window.at[pl.ds(14, 2)], -2, r),
        push(window.at[pl.ds(BELOW, 4)], window.at[pl.ds(2, 4)], 1, r),
        push(window.at[pl.ds(BELOW, 4)], window.at[pl.ds(10, 4)], -1, r),
    ]

    get_counts.wait()
    filled = c_s[0]
    lowest = d * FRAMES - BELOW
    used = [j < filled for j in range(CAP)]
    none = jnp.zeros((W, C), BF16)

    for box in (inc, act_one, grad_mid, act_two):
        for s in (OWN, NEAR, FAR):
            box[s, 0] = none
            box[s, CAP + 1] = none
    get_raw.wait()
    for j in range(CAP):
        inc[OWN, 1 + j] = jnp.where(used[j], raw[j], none)

    end = jnp.clip(filled - 1, 0, CAP - 1)
    last[0] = raw[end]
    inc_slots = send_slots(inc)
    edges = (
        push(last.at[0], inc_edge.at[0, OWN], 1, r),
        push(inc.at[OWN, 1], inc_edge.at[1, OWN], -1, r),
    )
    inc_edges = [edges]
    get_frames.wait()
    get_weights.wait()
    def products(fields, w, s, back, c, depths):
        tap = (1, near_tap, far_tap)[s]
        if back:
            tile = jnp.concatenate([w[2 - a, 2 - tap, 2 - c] for a in depths], axis=1)
            dims = (((1,), (1,)), ((), ()))
        else:
            tile = jnp.concatenate([w[a, tap, c] for a in depths], axis=0)
            dims = (((1,), (0,)), ((), ()))
        return lax.dot_general(fields, tile, dims, preferred_element_type=F32)

    def inner(slots, box, w, back, s):
        def step():
            if s != OWN:
                slots[s][0].wait_recv()
            fields = jnp.concatenate(
                [box[s, a : a + CAP].reshape(CAP * W, C) for a in range(3)], axis=1
            )
            for c in range(3):
                term = products(fields, w, s, back, c, (0, 1, 2))
                if s == OWN:
                    parts[c] = term.reshape(CAP, W, C)
                else:
                    parts[c] += term.reshape(CAP, W, C)

        when(far_there if s == FAR else None, step)
        if s != OWN:
            slots[s][4] = False

    def border(edges, edge, w, back, s):
        landed(*edges[s])
        there = far_there if s == FAR else None
        first_edge = jnp.where(both(exists(-1), there), edge[0, s], none)
        after_edge = jnp.where(both(exists(1), there), edge[1, s], none)
        for c in range(3):
            for side, field, depth in ((0, first_edge, 0), (1, after_edge, 2)):
                term = products(field, w, s, back, c, (depth,))
                if s == OWN:
                    fringe[side, c] = term
                else:
                    fringe[side, c] += term

    column = lax.broadcasted_iota(jnp.int32, (W, C), 0)

    def shifted(lower, centre, upper):
        lower = jnp.where(column == 0, 0.0, pltpu.roll(lower, 1, 0))
        upper = jnp.where(column == W - 1, 0.0, pltpu.roll(upper, W - 1, 0))
        return lower + centre + upper

    def slot(j):
        return shifted(parts[0, j], parts[1, j], parts[2, j])

    def inners(slots, box, w, back):
        for s in (OWN, NEAR, FAR):
            inner(slots, box, w, back, s)

    def borders(edges, edge, w, back):
        for s in (OWN, NEAR, FAR):
            border(edges, edge, w, back, s)
        return (shifted(*(fringe[side, c] for c in range(3))) for side in range(2))

    def patched(value, j, start, stop):
        if j == 0:
            value = value + start
        return value + jnp.where(filled == j + 1, stop, 0.0)

    for j in range(CAP):
        tap_at = [f_s[k, j] - lowest for k in range(TAPS)]
        tap_by = [jnp.where(used[j], w_s[k, j], 0.0) for k in range(TAPS)]
        for f in range(WINDOW):
            weight = jnp.float32(0.0)
            for k in range(TAPS):
                weight += jnp.where(tap_at[k] == f, tap_by[k], 0.0)
            mix[j, f] = weight

    get_two.wait()
    inner(inc_slots, inc, w_two, True, OWN)
    inner(inc_slots, inc, w_two, True, NEAR)
    inner(inc_slots, inc, w_two, True, FAR)
    for j in range(CAP):
        back_two[j] = slot(j)
    landed(*sources)

    def blend(j):
        summed = jnp.zeros((W, C), F32)
        for k in range(TAPS):
            at = jnp.clip(f_s[k, j] - lowest, 0, WINDOW - 1)
            summed += w_s[k, j] * window[at].astype(F32)
        return summed.astype(BF16)

    def silu(value):
        wide = value.astype(F32)
        return (wide * jax.nn.sigmoid(wide)).astype(BF16)

    value = blend(0)
    blended[0] = value
    act_one[OWN, 1] = silu(value)
    last[1] = silu(blend(end))
    act_one_edges = send_edges(act_one, act_one_edge, last.at[1])
    for j in range(1, CAP):
        value = jnp.where(used[j], blend(j), none)
        blended[j] = value
        act_one[OWN, 1 + j] = silu(value)
    act_one_slots = send_slots(act_one)

    landed(*edges)
    for s, row in ((NEAR, near), (FAR, far)):
        inc_edges.append(
            [
                push(inc_edge.at[k, OWN], inc_edge.at[k, s], 0, row, exists((-1, 1)[k]))
                for k in range(2)
            ]
        )

    def slope(value):
        wide = value.astype(F32)
        gate = jax.nn.sigmoid(wide)
        return gate * (1.0 + wide * (1.0 - gate))

    for j in range(CAP):
        slope_one[j] = slope(blended[j])

    def grad_at(j, value):
        return (raw[j].astype(F32) + slope(value) * back_two[j]).astype(BF16)

    get_one.wait()
    get_b_one.wait()
    get_b_two.wait()
    inner(act_one_slots, act_one, w_one, False, OWN)
    inner(act_one_slots, act_one, w_one, False, NEAR)
    start, stop = borders(inc_edges, inc_edge, w_two, True)
    for j in range(CAP):
        back_two[j] = patched(back_two[j], j, start, stop)
    inner(act_one_slots, act_one, w_one, False, FAR)
    start, stop = borders(act_one_edges, act_one_edge, w_one, False)

    def first_at(j, conv):
        return (conv + blended[j].astype(F32) + b_one[...]).astype(BF16)

    value = first_at(0, patched(slot(0), 0, start, stop))
    first[0] = value
    grad_mid[OWN, 1] = grad_at(0, value)
    value = first_at(end, slot(end) + stop + jnp.where(end == 0, start, 0.0))
    last[2] = grad_at(end, value)
    grad_mid_edges = send_edges(grad_mid, grad_mid_edge, last.at[2])
    last[3] = silu(value)
    for j in range(1, CAP):
        value = first_at(j, patched(slot(j), j, start, stop))
        value = jnp.where(used[j], value, none)
        first[j] = value
        grad_mid[OWN, 1 + j] = jnp.where(used[j], grad_at(j, value), none)
    grad_mid_slots = send_slots(grad_mid)
    for j in range(CAP):
        act_two[OWN, 1 + j] = silu(first[j])
    act_two_edges = send_edges(act_two, act_two_edge, last.at[3])
    act_two_slots = send_slots(act_two)

    inners(grad_mid_slots, grad_mid, w_one, True)
    start, stop = borders(grad_mid_edges, grad_mid_edge, w_one, True)
    for j in range(CAP):
        value = patched(slot(j), j, start, stop)
        low[j] = grad_mid[OWN, 1 + j].astype(F32) + slope_one[j] * value

    def gathered(f):
        summed = mix[0, f] * low[0]
        for j in range(1, CAP):
            summed += mix[j, f] * low[j]
        return summed

    spread_copies = []
    for head, count, at, by in ((0, 2, 8, -2), (14, 2, 10, 2), (2, 4, 0, -1), (10, 4, 4, 1)):
        for f in range(head, head + count):
            spread[f] = gathered(f).astype(BF16)
        spread_copies.append(push(spread.at[pl.ds(head, count)], arrived.at[pl.ds(at, count)], by, r))
    for f in range(FRAMES):
        source_grad[f] = gathered(BELOW + f)

    inners(act_two_slots, act_two, w_two, False)
    start, stop = borders(act_two_edges, act_two_edge, w_two, False)
    for j in range(CAP):
        value = patched(slot(j), j, start, stop) + first[j].astype(F32) + b_two[...]
        decoded[j] = jnp.where(used[j], value, 0.0).astype(BF16)

    landed(*spread_copies)
    for f in range(FRAMES):
        value = source_grad[f]
        value += jnp.where(exists(1), arrived[f].astype(F32), 0.0)
        value += jnp.where(exists(-1), arrived[4 + f].astype(F32), 0.0)
        if f >= 2:
            value += jnp.where(exists(2), arrived[8 + f - 2].astype(F32), 0.0)
        else:
            value += jnp.where(exists(-2), arrived[10 + f].astype(F32), 0.0)
        source_grad[f] = value
    left(*copies)


def finish(decoded_in, grad_in, decoded, source_grad, done):
    one = pltpu.make_async_copy(decoded_in, decoded, done.at[0])
    two = pltpu.make_async_copy(grad_in, source_grad, done.at[1])
    one.start()
    two.start()
    one.wait()
    two.wait()


def solution(mesh):
    spans, lines = mesh.shape["tm"], mesh.shape["rows"]

    def body(
        source,
        frame_counts,
        tap_frames,
        tap_weights,
        kernel_one,
        bias_one,
        kernel_two,
        bias_two,
        upstream,
    ):
        box = pltpu.VMEM((3, CAP + 2, W, C), BF16)
        edge = pltpu.VMEM((2, 3, W, C), BF16)
        slots = pltpu.VMEM((CAP, W, C), BF16)
        wide_slots = pltpu.VMEM((CAP, W, C), F32)
        kernels = pltpu.VMEM((3, 3, 3, C, C), BF16)
        bias = pltpu.VMEM((1, C), F32)
        decoded, source_grad = pl.pallas_call(
            lambda *refs: kernel(spans, lines, *refs),
            out_shape=(
                pltpu.VMEM((CAP, W, C), BF16),
                pltpu.VMEM((FRAMES, W, C), F32),
            ),
            in_specs=[pl.BlockSpec(memory_space=pl.ANY)] * 9,
            out_specs=[pl.BlockSpec(memory_space=pltpu.VMEM)] * 2,
            scratch_shapes=[
                pltpu.VMEM((WINDOW, W, C), BF16),
                kernels,
                kernels,
                bias,
                bias,
                slots,
                slots,
                slots,
                wide_slots,
                wide_slots,
                wide_slots,
                pltpu.VMEM((3, CAP, W, C), F32),
                pltpu.VMEM((2, 3, W, C), F32),
                box,
                box,
                box,
                box,
                edge,
                edge,
                edge,
                edge,
                pltpu.VMEM((4, W, C), BF16),
                pltpu.VMEM((WINDOW, W, C), BF16),
                pltpu.VMEM((12, W, C), BF16),
                pltpu.SMEM((CAP, WINDOW), F32),
                pltpu.SMEM((1,), jnp.int32),
                pltpu.SMEM((TAPS, CAP), jnp.int32),
                pltpu.SMEM((TAPS, CAP), F32),
                pltpu.SemaphoreType.DMA((9,)),
                pltpu.SemaphoreType.DMA((40,)),
                pltpu.SemaphoreType.DMA((40,)),
            ],
            compiler_params=pltpu.CompilerParams(
                collective_id=0, has_side_effects=True, vmem_limit_bytes=48 * 1024 * 1024
            ),
            cost_estimate=pl.CostEstimate(
                flops=4 * 2 * CAP * W * 27 * C * C,
                bytes_accessed=2 * 27 * C * C * 2,
                transcendentals=0,
            ),
        )(
            *(
                x if x is frame_counts else pltpu.with_memory_space_constraint(x, pltpu.HBM)
                for x in (
                    source.reshape(FRAMES, W, C),
                    frame_counts,
                    tap_frames.T,
                    tap_weights.T,
                    kernel_one,
                    bias_one.reshape(1, C),
                    kernel_two,
                    bias_two.reshape(1, C),
                    upstream.reshape(CAP, W, C),
                )
            )
        )
        decoded, source_grad = pl.pallas_call(
            finish,
            out_shape=(
                jax.ShapeDtypeStruct((CAP, W, C), BF16),
                jax.ShapeDtypeStruct((FRAMES, W, C), F32),
            ),
            in_specs=[pl.BlockSpec(memory_space=pltpu.VMEM)] * 2,
            out_specs=[pl.BlockSpec(memory_space=pl.ANY)] * 2,
            scratch_shapes=[pltpu.SemaphoreType.DMA((2,))],
        )(*(pltpu.with_memory_space_constraint(x, pltpu.VMEM) for x in (decoded, source_grad)))
        return decoded.reshape(CAP, 1, W, C), source_grad.reshape(FRAMES, 1, W, C)

    whole = P("tm", "rows", None, None)
    return jax.shard_map(
        body,
        mesh=mesh,
        in_specs=(whole, P("tm"), P("tm", None), P("tm", None), P(), P(), P(), P(), whole),
        out_specs=(whole, whole),
        check_vma=False,
    )
```

```python
import jax
import jax.numpy as jnp
from jax import lax
from jax.experimental import pallas as pl
from jax.experimental.pallas import tpu as pltpu
from jax.sharding import PartitionSpec as P

MESH = pl.DeviceIdType.MESH
FRAMES = 4
CAP = 9
TAPS = 4
WINDOW = 16
BELOW = 6
W = 32
C = 256
OWN, NEAR, FAR = 0, 1, 2
BF16 = jnp.bfloat16
F32 = jnp.float32


def kernel(
    spans,
    lines,
    source,
    counts,
    frames,
    weights,
    kernel_one,
    bias_one,
    kernel_two,
    bias_two,
    upstream,
    decoded,
    source_grad,
    window,
    w_one,
    w_two,
    b_one,
    b_two,
    raw,
    blended,
    first,
    low,
    back_two,
    slope_one,
    parts,
    fringe,
    partial,
    inc,
    act_one,
    grad_mid,
    act_two,
    inc_edge,
    act_one_edge,
    grad_mid_edge,
    act_two_edge,
    last,
    spread,
    arrived,
    mix,
    c_s,
    f_s,
    w_s,
    local,
    send,
    recv,
):
    d = lax.axis_index("tm")
    r = lax.axis_index("rows")
    odd = lax.rem(r, 2)
    near = r + 1 - 2 * odd
    far = lax.rem(r - 1 + 2 * odd + lines, lines)
    far_there = jnp.where(odd == 0, r > 0, r < lines - 1)
    near_tap = 2 - 2 * odd
    far_tap = 2 * odd

    upper = spans - 1

    def exists(by):
        if by == 0:
            return None
        return d >= -by if by < 0 else d <= upper - by

    def both(one, two):
        if one is None or two is None:
            return two if one is None else one
        return one & two

    def when(condition, action):
        if condition is None:
            action()
        else:
            pl.when(condition)(action)

    def line(row):
        return far_there if row is far else None

    reach = [(by, r) for by in (-2, -1, 1, 2)] + [(0, near), (0, far)]
    barrier = pltpu.get_barrier_semaphore()
    greeted = jnp.int32(0)
    for by, row in reach:
        there = both(exists(by), line(row))

        def greet(by=by, row=row):
            pl.semaphore_signal(
                barrier, inc=1, device_id={"tm": d + by, "rows": row}, device_id_type=MESH
            )

        when(there, greet)
        greeted += 1 if there is None else jnp.where(there, 1, 0)

    def fetch(k, src, dst):
        copy = pltpu.make_async_copy(src, dst, local.at[k])
        copy.start()
        fetched.append(copy)
        return copy

    fetched = []
    get_source = fetch(0, source, window.at[pl.ds(BELOW, FRAMES)])
    get_raw = fetch(4, upstream, raw)
    get_counts = fetch(1, counts, c_s)
    get_frames = fetch(2, frames, f_s)
    get_weights = fetch(3, weights, w_s)
    get_two = fetch(5, kernel_two, w_two)
    get_one = fetch(6, kernel_one, w_one)
    get_b_one = fetch(7, bias_one, b_one)
    get_b_two = fetch(8, bias_two, b_two)

    copies = []

    def push(src, dst, by, row, held=None, now=True):
        k = len(copies)
        copy = pltpu.make_async_remote_copy(
            src_ref=src,
            dst_ref=dst,
            send_sem=send.at[k],
            recv_sem=recv.at[k],
            device_id={"tm": d + by, "rows": row},
            device_id_type=MESH,
        )
        sent = both(both(exists(by), line(row)), held)
        if now:
            when(sent, copy.start)
        entry = [copy, sent, both(both(exists(-by), line(row)), held), True, True]
        copies.append(entry)
        return entry

    def landed(*entries):
        for entry in entries:
            if entry[4]:
                when(entry[2], entry[0].wait_recv)
                entry[4] = False

    def left(*entries):
        for entry in entries:
            if entry[3]:
                when(entry[1], entry[0].wait_send)
                entry[3] = False

    def send_edges(box, edge, ends):
        edges = [None] * 3
        for s, row in ((FAR, far), (OWN, r), (NEAR, near)):
            edges[s] = (
                push(ends, edge.at[0, s], 1, row, now=False),
                push(box.at[OWN, 1], edge.at[1, s], -1, row, now=False),
            )
        for side, by in ((0, 1), (1, -1)):

            def start(side=side):
                when(far_there, edges[FAR][side][0].start)
                edges[OWN][side][0].start()
                edges[NEAR][side][0].start()

            when(exists(by), start)
        return edges

    def send_slots(box):
        mine = box.at[OWN, pl.ds(1, CAP)]
        far_mine = push(mine, box.at[FAR, pl.ds(1, CAP)], 0, far)
        near_mine = push(mine, box.at[NEAR, pl.ds(1, CAP)], 0, near)
        return None, near_mine, far_mine

    get_source.wait()
    pl.semaphore_wait(barrier, greeted)
    sources = [
        push(window.at[pl.ds(BELOW + 2, 2)], window.at[pl.ds(0, 2)], 2, r),
        push(window.at[pl.ds(BELOW, 2)], window.at[pl.ds(14, 2)], -2, r),
        push(window.at[pl.ds(BELOW, 4)], window.at[pl.ds(2, 4)], 1, r),
        push(window.at[pl.ds(BELOW, 4)], window.at[pl.ds(10, 4)], -1, r),
    ]

    get_counts.wait()
    filled = c_s[0]
    lowest = d * FRAMES - BELOW
    used = [j < filled for j in range(CAP)]
    none = jnp.zeros((W, C), BF16)

    for box in (inc, act_one, grad_mid, act_two):
        for s in (OWN, NEAR, FAR):
            box[s, 0] = none
            box[s, CAP + 1] = none
    get_raw.wait()
    for j in range(CAP):
        inc[OWN, 1 + j] = jnp.where(used[j], raw[j], none)

    end = jnp.clip(filled - 1, 0, CAP - 1)
    last[0] = raw[end]
    inc_slots = send_slots(inc)
    edges = (
        push(last.at[0], inc_edge.at[0, OWN], 1, r),
        push(inc.at[OWN, 1], inc_edge.at[1, OWN], -1, r),
    )
    inc_edges = [edges]
    get_frames.wait()
    get_weights.wait()
    def products(fields, w, s, back, c, depths):
        tap = (1, near_tap, far_tap)[s]
        if back:
            tile = jnp.concatenate([w[2 - a, 2 - tap, 2 - c] for a in depths], axis=1)
            dims = (((1,), (1,)), ((), ()))
        else:
            tile = jnp.concatenate([w[a, tap, c] for a in depths], axis=0)
            dims = (((1,), (0,)), ((), ()))
        return lax.dot_general(fields, tile, dims, preferred_element_type=F32)

    def inner(slots, box, w, back, s):
        def step():
            if s != OWN:
                slots[s][0].wait_recv()
            fields = jnp.concatenate(
                [box[s, a : a + CAP].reshape(CAP * W, C) for a in range(3)], axis=1
            )
            for c in range(3):
                term = products(fields, w, s, back, c, (0, 1, 2))
                if s == OWN:
                    parts[c] = term.reshape(CAP, W, C)
                else:
                    parts[c] += term.reshape(CAP, W, C)

        when(far_there if s == FAR else None, step)
        if s != OWN:
            slots[s][4] = False

    def border(edges, edge, w, back, s):
        landed(*edges[s])
        there = far_there if s == FAR else None
        first_edge = jnp.where(both(exists(-1), there), edge[0, s], none)
        after_edge = jnp.where(both(exists(1), there), edge[1, s], none)
        for c in range(3):
            for side, field, depth in ((0, first_edge, 0), (1, after_edge, 2)):
                term = products(field, w, s, back, c, (depth,))
                if s == OWN:
                    fringe[side, c] = term
                else:
                    fringe[side, c] += term

    column = lax.broadcasted_iota(jnp.int32, (W, C), 0)

    def shifted(lower, centre, upper):
        lower = jnp.where(column == 0, 0.0, pltpu.roll(lower, 1, 0))
        upper = jnp.where(column == W - 1, 0.0, pltpu.roll(upper, W - 1, 0))
        return lower + centre + upper

    def slot(j):
        return shifted(parts[0, j], parts[1, j], parts[2, j])

    def inners(slots, box, w, back):
        for s in (OWN, NEAR, FAR):
            inner(slots, box, w, back, s)

    def borders(edges, edge, w, back):
        for s in (OWN, NEAR, FAR):
            border(edges, edge, w, back, s)
        return (shifted(*(fringe[side, c] for c in range(3))) for side in range(2))

    def patched(value, j, start, stop):
        if j == 0:
            value = value + start
        return value + jnp.where(filled == j + 1, stop, 0.0)

    for j in range(CAP):
        tap_at = [f_s[k, j] - lowest for k in range(TAPS)]
        tap_by = [jnp.where(used[j], w_s[k, j], 0.0) for k in range(TAPS)]
        for f in range(WINDOW):
            weight = jnp.float32(0.0)
            for k in range(TAPS):
                weight += jnp.where(tap_at[k] == f, tap_by[k], 0.0)
            mix[j, f] = weight

    get_two.wait()
    inner(inc_slots, inc, w_two, True, OWN)
    inner(inc_slots, inc, w_two, True, NEAR)
    inner(inc_slots, inc, w_two, True, FAR)
    for j in range(CAP):
        back_two[j] = slot(j)
    landed(*sources)

    def blend(j):
        summed = jnp.zeros((W, C), F32)
        for k in range(TAPS):
            at = jnp.clip(f_s[k, j] - lowest, 0, WINDOW - 1)
            summed += w_s[k, j] * window[at].astype(F32)
        return summed.astype(BF16)

    def silu(value):
        wide = value.astype(F32)
        return (wide * jax.nn.sigmoid(wide)).astype(BF16)

    value = blend(0)
    blended[0] = value
    act_one[OWN, 1] = silu(value)
    last[1] = silu(blend(end))
    act_one_edges = send_edges(act_one, act_one_edge, last.at[1])
    for j in range(1, CAP):
        value = jnp.where(used[j], blend(j), none)
        blended[j] = value
        act_one[OWN, 1 + j] = silu(value)
    act_one_slots = send_slots(act_one)

    landed(*edges)
    for s, row in ((NEAR, near), (FAR, far)):
        inc_edges.append(
            [
                push(inc_edge.at[k, OWN], inc_edge.at[k, s], 0, row, exists((-1, 1)[k]))
                for k in range(2)
            ]
        )

    def slope(value):
        wide = value.astype(F32)
        gate = jax.nn.sigmoid(wide)
        return gate * (1.0 + wide * (1.0 - gate))

    for j in range(CAP):
        slope_one[j] = slope(blended[j])

    def grad_at(j, value):
        return (raw[j].astype(F32) + slope(value) * back_two[j]).astype(BF16)

    get_one.wait()
    get_b_one.wait()
    get_b_two.wait()
    inner(act_one_slots, act_one, w_one, False, OWN)
    inner(act_one_slots, act_one, w_one, False, NEAR)
    start, stop = borders(inc_edges, inc_edge, w_two, True)
    for j in range(CAP):
        back_two[j] = patched(back_two[j], j, start, stop)
    inner(act_one_slots, act_one, w_one, False, FAR)
    start, stop = borders(act_one_edges, act_one_edge, w_one, False)

    def first_at(j, conv):
        return (conv + blended[j].astype(F32) + b_one[...]).astype(BF16)

    value = first_at(0, patched(slot(0), 0, start, stop))
    first[0] = value
    grad_mid[OWN, 1] = grad_at(0, value)
    value = first_at(end, slot(end) + stop + jnp.where(end == 0, start, 0.0))
    last[2] = grad_at(end, value)
    grad_mid_edges = send_edges(grad_mid, grad_mid_edge, last.at[2])
    last[3] = silu(value)
    for j in range(1, CAP):
        value = first_at(j, patched(slot(j), j, start, stop))
        value = jnp.where(used[j], value, none)
        first[j] = value
        grad_mid[OWN, 1 + j] = jnp.where(used[j], grad_at(j, value), none)
    grad_mid_slots = send_slots(grad_mid)
    for j in range(CAP):
        act_two[OWN, 1 + j] = silu(first[j])
    act_two_edges = send_edges(act_two, act_two_edge, last.at[3])
    act_two_slots = send_slots(act_two)

    inners(grad_mid_slots, grad_mid, w_one, True)
    for j in range(CAP):
        low[j] = grad_mid[OWN, 1 + j].astype(F32) + slope_one[j] * slot(j)
    for f in range(WINDOW):
        summed = mix[0, f] * low[0]
        for j in range(1, CAP):
            summed += mix[j, f] * low[j]
        partial[f] = summed
    start, stop = borders(grad_mid_edges, grad_mid_edge, w_one, True)
    start = slope_one[0] * start
    stop = slope_one[end] * stop

    def gathered(f):
        return partial[f] + mix[0, f] * start + mix[end, f] * stop

    spread_copies = []
    for head, count, at, by in ((0, 2, 8, -2), (14, 2, 10, 2), (2, 4, 0, -1), (10, 4, 4, 1)):
        for f in range(head, head + count):
            spread[f] = gathered(f).astype(BF16)
        spread_copies.append(push(spread.at[pl.ds(head, count)], arrived.at[pl.ds(at, count)], by, r))
    for f in range(FRAMES):
        source_grad[f] = gathered(BELOW + f)

    inners(act_two_slots, act_two, w_two, False)
    start, stop = borders(act_two_edges, act_two_edge, w_two, False)
    for j in range(CAP):
        value = patched(slot(j), j, start, stop) + first[j].astype(F32) + b_two[...]
        decoded[j] = jnp.where(used[j], value, 0.0).astype(BF16)
    left(*copies)
    landed(*spread_copies)
    for f in range(FRAMES):
        value = source_grad[f]
        value += jnp.where(exists(1), arrived[f].astype(F32), 0.0)
        value += jnp.where(exists(-1), arrived[4 + f].astype(F32), 0.0)
        if f >= 2:
            value += jnp.where(exists(2), arrived[8 + f - 2].astype(F32), 0.0)
        else:
            value += jnp.where(exists(-2), arrived[10 + f].astype(F32), 0.0)
        source_grad[f] = value


def finish(decoded_in, grad_in, decoded, source_grad, done):
    one = pltpu.make_async_copy(decoded_in, decoded, done.at[0])
    two = pltpu.make_async_copy(grad_in, source_grad, done.at[1])
    one.start()
    two.start()
    one.wait()
    two.wait()


def solution(mesh):
    spans, lines = mesh.shape["tm"], mesh.shape["rows"]

    def body(
        source,
        frame_counts,
        tap_frames,
        tap_weights,
        kernel_one,
        bias_one,
        kernel_two,
        bias_two,
        upstream,
    ):
        box = pltpu.VMEM((3, CAP + 2, W, C), BF16)
        edge = pltpu.VMEM((2, 3, W, C), BF16)
        slots = pltpu.VMEM((CAP, W, C), BF16)
        wide_slots = pltpu.VMEM((CAP, W, C), F32)
        kernels = pltpu.VMEM((3, 3, 3, C, C), BF16)
        bias = pltpu.VMEM((1, C), F32)
        decoded, source_grad = pl.pallas_call(
            lambda *refs: kernel(spans, lines, *refs),
            out_shape=(
                pltpu.VMEM((CAP, W, C), BF16),
                pltpu.VMEM((FRAMES, W, C), F32),
            ),
            in_specs=[pl.BlockSpec(memory_space=pl.ANY)] * 9,
            out_specs=[pl.BlockSpec(memory_space=pltpu.VMEM)] * 2,
            scratch_shapes=[
                pltpu.VMEM((WINDOW, W, C), BF16),
                kernels,
                kernels,
                bias,
                bias,
                slots,
                slots,
                slots,
                wide_slots,
                wide_slots,
                wide_slots,
                pltpu.VMEM((3, CAP, W, C), F32),
                pltpu.VMEM((2, 3, W, C), F32),
                pltpu.VMEM((WINDOW, W, C), F32),
                box,
                box,
                box,
                box,
                edge,
                edge,
                edge,
                edge,
                pltpu.VMEM((4, W, C), BF16),
                pltpu.VMEM((WINDOW, W, C), BF16),
                pltpu.VMEM((12, W, C), BF16),
                pltpu.SMEM((CAP, WINDOW), F32),
                pltpu.SMEM((1,), jnp.int32),
                pltpu.SMEM((TAPS, CAP), jnp.int32),
                pltpu.SMEM((TAPS, CAP), F32),
                pltpu.SemaphoreType.DMA((9,)),
                pltpu.SemaphoreType.DMA((40,)),
                pltpu.SemaphoreType.DMA((40,)),
            ],
            compiler_params=pltpu.CompilerParams(
                collective_id=0, has_side_effects=True, vmem_limit_bytes=48 * 1024 * 1024
            ),
            cost_estimate=pl.CostEstimate(
                flops=4 * 2 * CAP * W * 27 * C * C,
                bytes_accessed=2 * 27 * C * C * 2,
                transcendentals=0,
            ),
        )(
            *(
                x if x is frame_counts else pltpu.with_memory_space_constraint(x, pltpu.HBM)
                for x in (
                    source.reshape(FRAMES, W, C),
                    frame_counts,
                    tap_frames.T,
                    tap_weights.T,
                    kernel_one,
                    bias_one.reshape(1, C),
                    kernel_two,
                    bias_two.reshape(1, C),
                    upstream.reshape(CAP, W, C),
                )
            )
        )
        decoded, source_grad = pl.pallas_call(
            finish,
            out_shape=(
                jax.ShapeDtypeStruct((CAP, W, C), BF16),
                jax.ShapeDtypeStruct((FRAMES, W, C), F32),
            ),
            in_specs=[pl.BlockSpec(memory_space=pltpu.VMEM)] * 2,
            out_specs=[pl.BlockSpec(memory_space=pl.ANY)] * 2,
            scratch_shapes=[pltpu.SemaphoreType.DMA((2,))],
        )(*(pltpu.with_memory_space_constraint(x, pltpu.VMEM) for x in (decoded, source_grad)))
        return decoded.reshape(CAP, 1, W, C), source_grad.reshape(FRAMES, 1, W, C)

    whole = P("tm", "rows", None, None)
    return jax.shard_map(
        body,
        mesh=mesh,
        in_specs=(whole, P("tm"), P("tm", None), P("tm", None), P(), P(), P(), P(), whole),
        out_specs=(whole, whole),
        check_vma=False,
    )
```

```python
import jax
import jax.numpy as jnp
from jax import lax
from jax.experimental import pallas as pl
from jax.experimental.pallas import tpu as pltpu
from jax.sharding import PartitionSpec as P

MESH = pl.DeviceIdType.MESH
FRAMES = 4
CAP = 9
TAPS = 4
WINDOW = 16
BELOW = 6
W = 32
C = 256
OWN, NEAR, FAR = 0, 1, 2
BF16 = jnp.bfloat16
F32 = jnp.float32


def kernel(
    spans,
    lines,
    source,
    counts,
    frames,
    weights,
    kernel_one,
    bias_one,
    kernel_two,
    bias_two,
    upstream,
    decoded,
    source_grad,
    window,
    w_one,
    w_two,
    b_one,
    b_two,
    raw,
    blended,
    first,
    low,
    back_two,
    slope_one,
    parts,
    fringe,
    partial,
    inc,
    act_one,
    grad_mid,
    act_two,
    inc_edge,
    act_one_edge,
    grad_mid_edge,
    act_two_edge,
    last,
    spread,
    arrived,
    mix,
    c_s,
    f_s,
    w_s,
    local,
    send,
    recv,
):
    d = lax.axis_index("tm")
    r = lax.axis_index("rows")
    odd = lax.rem(r, 2)
    near = r + 1 - 2 * odd
    far = lax.rem(r - 1 + 2 * odd + lines, lines)
    far_there = jnp.where(odd == 0, r > 0, r < lines - 1)
    near_tap = 2 - 2 * odd
    far_tap = 2 * odd

    upper = spans - 1

    def exists(by):
        if by == 0:
            return None
        return d >= -by if by < 0 else d <= upper - by

    def both(one, two):
        if one is None or two is None:
            return two if one is None else one
        return one & two

    def when(condition, action):
        if condition is None:
            action()
        else:
            pl.when(condition)(action)

    def line(row):
        return far_there if row is far else None

    reach = [(by, r) for by in (-2, -1, 1, 2)] + [(0, near), (0, far)]
    barrier = pltpu.get_barrier_semaphore()
    greeted = jnp.int32(0)
    for by, row in reach:
        there = both(exists(by), line(row))

        def greet(by=by, row=row):
            pl.semaphore_signal(
                barrier, inc=1, device_id={"tm": d + by, "rows": row}, device_id_type=MESH
            )

        when(there, greet)
        greeted += 1 if there is None else jnp.where(there, 1, 0)

    def fetch(k, src, dst):
        copy = pltpu.make_async_copy(src, dst, local.at[k])
        copy.start()
        fetched.append(copy)
        return copy

    fetched = []
    get_source = fetch(0, source, window.at[pl.ds(BELOW, FRAMES)])
    get_raw = fetch(4, upstream, raw)
    get_counts = fetch(1, counts, c_s)
    get_frames = fetch(2, frames, f_s)
    get_weights = fetch(3, weights, w_s)
    get_two = fetch(5, kernel_two, w_two)
    get_one = fetch(6, kernel_one, w_one)
    get_b_one = fetch(7, bias_one, b_one)
    get_b_two = fetch(8, bias_two, b_two)

    copies = []

    def push(src, dst, by, row, held=None, now=True):
        k = len(copies)
        copy = pltpu.make_async_remote_copy(
            src_ref=src,
            dst_ref=dst,
            send_sem=send.at[k],
            recv_sem=recv.at[k],
            device_id={"tm": d + by, "rows": row},
            device_id_type=MESH,
        )
        sent = both(both(exists(by), line(row)), held)
        if now:
            when(sent, copy.start)
        entry = [copy, sent, both(both(exists(-by), line(row)), held), True, True]
        copies.append(entry)
        return entry

    def landed(*entries):
        for entry in entries:
            if entry[4]:
                when(entry[2], entry[0].wait_recv)
                entry[4] = False

    def left(*entries):
        for entry in entries:
            if entry[3]:
                when(entry[1], entry[0].wait_send)
                entry[3] = False

    def send_edges(box, edge, ends):
        edges = [None] * 3
        for s, row in ((FAR, far), (OWN, r), (NEAR, near)):
            edges[s] = (
                push(ends, edge.at[0, s], 1, row, now=False),
                push(box.at[OWN, 1], edge.at[1, s], -1, row, now=False),
            )
        for side, by in ((0, 1), (1, -1)):

            def start(side=side):
                edges[OWN][side][0].start()
                edges[NEAR][side][0].start()
                when(far_there, edges[FAR][side][0].start)

            when(exists(by), start)
        return edges

    def send_slots(box):
        mine = box.at[OWN, pl.ds(1, CAP)]
        far_mine = push(mine, box.at[FAR, pl.ds(1, CAP)], 0, far)
        near_mine = push(mine, box.at[NEAR, pl.ds(1, CAP)], 0, near)
        return None, near_mine, far_mine

    get_source.wait()
    pl.semaphore_wait(barrier, greeted)
    sources = [
        push(window.at[pl.ds(BELOW + 2, 2)], window.at[pl.ds(0, 2)], 2, r),
        push(window.at[pl.ds(BELOW, 2)], window.at[pl.ds(14, 2)], -2, r),
        push(window.at[pl.ds(BELOW, 4)], window.at[pl.ds(2, 4)], 1, r),
        push(window.at[pl.ds(BELOW, 4)], window.at[pl.ds(10, 4)], -1, r),
    ]

    get_counts.wait()
    filled = c_s[0]
    lowest = d * FRAMES - BELOW
    used = [j < filled for j in range(CAP)]
    none = jnp.zeros((W, C), BF16)

    for box in (inc, act_one, grad_mid, act_two):
        for s in (OWN, NEAR, FAR):
            box[s, 0] = none
            box[s, CAP + 1] = none
    get_raw.wait()
    for j in range(CAP):
        inc[OWN, 1 + j] = jnp.where(used[j], raw[j], none)

    end = jnp.clip(filled - 1, 0, CAP - 1)
    last[0] = raw[end]
    inc_slots = send_slots(inc)
    edges = (
        push(last.at[0], inc_edge.at[0, OWN], 1, r),
        push(inc.at[OWN, 1], inc_edge.at[1, OWN], -1, r),
    )
    inc_edges = [edges]
    get_frames.wait()
    get_weights.wait()
    def products(fields, w, s, back, c, depths):
        tap = (1, near_tap, far_tap)[s]
        if back:
            tile = jnp.concatenate([w[2 - a, 2 - tap, 2 - c] for a in depths], axis=1)
            dims = (((1,), (1,)), ((), ()))
        else:
            tile = jnp.concatenate([w[a, tap, c] for a in depths], axis=0)
            dims = (((1,), (0,)), ((), ()))
        return lax.dot_general(fields, tile, dims, preferred_element_type=F32)

    def inner(slots, box, w, back, s):
        def step():
            if s != OWN:
                slots[s][0].wait_recv()
            fields = jnp.concatenate(
                [box[s, a : a + CAP].reshape(CAP * W, C) for a in range(3)], axis=1
            )
            for c in range(3):
                term = products(fields, w, s, back, c, (0, 1, 2))
                if s == OWN:
                    parts[c] = term.reshape(CAP, W, C)
                else:
                    parts[c] += term.reshape(CAP, W, C)

        when(far_there if s == FAR else None, step)
        if s != OWN:
            slots[s][4] = False

    def border(edges, edge, w, back, s):
        landed(*edges[s])
        there = far_there if s == FAR else None
        first_edge = jnp.where(both(exists(-1), there), edge[0, s], none)
        after_edge = jnp.where(both(exists(1), there), edge[1, s], none)
        for c in range(3):
            for side, field, depth in ((0, first_edge, 0), (1, after_edge, 2)):
                term = products(field, w, s, back, c, (depth,))
                if s == OWN:
                    fringe[side, c] = term
                else:
                    fringe[side, c] += term

    column = lax.broadcasted_iota(jnp.int32, (W, C), 0)

    def shifted(lower, centre, upper):
        lower = jnp.where(column == 0, 0.0, pltpu.roll(lower, 1, 0))
        upper = jnp.where(column == W - 1, 0.0, pltpu.roll(upper, W - 1, 0))
        return lower + centre + upper

    def slot(j):
        return shifted(parts[0, j], parts[1, j], parts[2, j])

    def inners(slots, box, w, back):
        for s in (OWN, NEAR, FAR):
            inner(slots, box, w, back, s)

    def borders(edges, edge, w, back):
        for s in (OWN, NEAR, FAR):
            border(edges, edge, w, back, s)
        return (shifted(*(fringe[side, c] for c in range(3))) for side in range(2))

    def patched(value, j, start, stop):
        if j == 0:
            value = value + start
        return value + jnp.where(filled == j + 1, stop, 0.0)

    for j in range(CAP):
        tap_at = [f_s[k, j] - lowest for k in range(TAPS)]
        tap_by = [jnp.where(used[j], w_s[k, j], 0.0) for k in range(TAPS)]
        for f in range(WINDOW):
            weight = jnp.float32(0.0)
            for k in range(TAPS):
                weight += jnp.where(tap_at[k] == f, tap_by[k], 0.0)
            mix[j, f] = weight

    get_two.wait()
    inner(inc_slots, inc, w_two, True, OWN)
    inner(inc_slots, inc, w_two, True, NEAR)
    inner(inc_slots, inc, w_two, True, FAR)
    for j in range(CAP):
        back_two[j] = slot(j)
    landed(*sources)

    def blend(j):
        summed = jnp.zeros((W, C), F32)
        for k in range(TAPS):
            at = jnp.clip(f_s[k, j] - lowest, 0, WINDOW - 1)
            summed += w_s[k, j] * window[at].astype(F32)
        return summed.astype(BF16)

    def silu(value):
        wide = value.astype(F32)
        return (wide * jax.nn.sigmoid(wide)).astype(BF16)

    value = blend(0)
    blended[0] = value
    act_one[OWN, 1] = silu(value)
    last[1] = silu(blend(end))
    act_one_edges = send_edges(act_one, act_one_edge, last.at[1])
    landed(*edges)
    for s, row in ((NEAR, near), (FAR, far)):
        inc_edges.append(
            [
                push(inc_edge.at[k, OWN], inc_edge.at[k, s], 0, row, exists((-1, 1)[k]))
                for k in range(2)
            ]
        )
    for j in range(1, CAP):
        value = jnp.where(used[j], blend(j), none)
        blended[j] = value
        act_one[OWN, 1 + j] = silu(value)
    act_one_slots = send_slots(act_one)

    def slope(value):
        wide = value.astype(F32)
        gate = jax.nn.sigmoid(wide)
        return gate * (1.0 + wide * (1.0 - gate))

    for j in range(CAP):
        slope_one[j] = slope(blended[j])

    def grad_at(j, value):
        return (raw[j].astype(F32) + slope(value) * back_two[j]).astype(BF16)

    get_one.wait()
    get_b_one.wait()
    get_b_two.wait()
    inner(act_one_slots, act_one, w_one, False, OWN)
    inner(act_one_slots, act_one, w_one, False, NEAR)
    start, stop = borders(inc_edges, inc_edge, w_two, True)
    for j in range(CAP):
        back_two[j] = patched(back_two[j], j, start, stop)
    inner(act_one_slots, act_one, w_one, False, FAR)
    start, stop = borders(act_one_edges, act_one_edge, w_one, False)

    def first_at(j, conv):
        return (conv + blended[j].astype(F32) + b_one[...]).astype(BF16)

    value = first_at(0, patched(slot(0), 0, start, stop))
    first[0] = value
    grad_mid[OWN, 1] = grad_at(0, value)
    value = first_at(end, slot(end) + stop + jnp.where(end == 0, start, 0.0))
    last[2] = grad_at(end, value)
    grad_mid_edges = send_edges(grad_mid, grad_mid_edge, last.at[2])
    last[3] = silu(value)
    for j in range(1, CAP):
        value = first_at(j, patched(slot(j), j, start, stop))
        value = jnp.where(used[j], value, none)
        first[j] = value
        grad_mid[OWN, 1 + j] = jnp.where(used[j], grad_at(j, value), none)
    grad_mid_slots = send_slots(grad_mid)
    for j in range(CAP):
        act_two[OWN, 1 + j] = silu(first[j])
    act_two_edges = send_edges(act_two, act_two_edge, last.at[3])
    act_two_slots = send_slots(act_two)

    inners(grad_mid_slots, grad_mid, w_one, True)
    for j in range(CAP):
        low[j] = grad_mid[OWN, 1 + j].astype(F32) + slope_one[j] * slot(j)
    for f in range(WINDOW):
        summed = mix[0, f] * low[0]
        for j in range(1, CAP):
            summed += mix[j, f] * low[j]
        partial[f] = summed
    start, stop = borders(grad_mid_edges, grad_mid_edge, w_one, True)
    start = slope_one[0] * start
    stop = slope_one[end] * stop

    def gathered(f):
        return partial[f] + mix[0, f] * start + mix[end, f] * stop

    spread_copies = []
    for head, count, at, by in ((0, 2, 8, -2), (14, 2, 10, 2), (2, 4, 0, -1), (10, 4, 4, 1)):
        for f in range(head, head + count):
            spread[f] = gathered(f).astype(BF16)
        spread_copies.append(push(spread.at[pl.ds(head, count)], arrived.at[pl.ds(at, count)], by, r))
    for f in range(FRAMES):
        source_grad[f] = gathered(BELOW + f)

    inners(act_two_slots, act_two, w_two, False)
    start, stop = borders(act_two_edges, act_two_edge, w_two, False)
    for j in range(CAP):
        value = patched(slot(j), j, start, stop) + first[j].astype(F32) + b_two[...]
        decoded[j] = jnp.where(used[j], value, 0.0).astype(BF16)
    left(*copies)
    landed(*spread_copies)
    for f in range(FRAMES):
        value = source_grad[f]
        value += jnp.where(exists(1), arrived[f].astype(F32), 0.0)
        value += jnp.where(exists(-1), arrived[4 + f].astype(F32), 0.0)
        if f >= 2:
            value += jnp.where(exists(2), arrived[8 + f - 2].astype(F32), 0.0)
        else:
            value += jnp.where(exists(-2), arrived[10 + f].astype(F32), 0.0)
        source_grad[f] = value


def finish(decoded_in, grad_in, decoded, source_grad, done):
    one = pltpu.make_async_copy(decoded_in, decoded, done.at[0])
    two = pltpu.make_async_copy(grad_in, source_grad, done.at[1])
    one.start()
    two.start()
    one.wait()
    two.wait()


def solution(mesh):
    spans, lines = mesh.shape["tm"], mesh.shape["rows"]

    def body(
        source,
        frame_counts,
        tap_frames,
        tap_weights,
        kernel_one,
        bias_one,
        kernel_two,
        bias_two,
        upstream,
    ):
        box = pltpu.VMEM((3, CAP + 2, W, C), BF16)
        edge = pltpu.VMEM((2, 3, W, C), BF16)
        slots = pltpu.VMEM((CAP, W, C), BF16)
        wide_slots = pltpu.VMEM((CAP, W, C), F32)
        kernels = pltpu.VMEM((3, 3, 3, C, C), BF16)
        bias = pltpu.VMEM((1, C), F32)
        decoded, source_grad = pl.pallas_call(
            lambda *refs: kernel(spans, lines, *refs),
            out_shape=(
                pltpu.VMEM((CAP, W, C), BF16),
                pltpu.VMEM((FRAMES, W, C), F32),
            ),
            in_specs=[pl.BlockSpec(memory_space=pl.ANY)] * 9,
            out_specs=[pl.BlockSpec(memory_space=pltpu.VMEM)] * 2,
            scratch_shapes=[
                pltpu.VMEM((WINDOW, W, C), BF16),
                kernels,
                kernels,
                bias,
                bias,
                slots,
                slots,
                slots,
                wide_slots,
                wide_slots,
                wide_slots,
                pltpu.VMEM((3, CAP, W, C), F32),
                pltpu.VMEM((2, 3, W, C), F32),
                pltpu.VMEM((WINDOW, W, C), F32),
                box,
                box,
                box,
                box,
                edge,
                edge,
                edge,
                edge,
                pltpu.VMEM((4, W, C), BF16),
                pltpu.VMEM((WINDOW, W, C), BF16),
                pltpu.VMEM((12, W, C), BF16),
                pltpu.SMEM((CAP, WINDOW), F32),
                pltpu.SMEM((1,), jnp.int32),
                pltpu.SMEM((TAPS, CAP), jnp.int32),
                pltpu.SMEM((TAPS, CAP), F32),
                pltpu.SemaphoreType.DMA((9,)),
                pltpu.SemaphoreType.DMA((40,)),
                pltpu.SemaphoreType.DMA((40,)),
            ],
            compiler_params=pltpu.CompilerParams(
                collective_id=0, has_side_effects=True, vmem_limit_bytes=48 * 1024 * 1024
            ),
            cost_estimate=pl.CostEstimate(
                flops=4 * 2 * CAP * W * 27 * C * C,
                bytes_accessed=2 * 27 * C * C * 2,
                transcendentals=0,
            ),
        )(
            *(
                x if x is frame_counts else pltpu.with_memory_space_constraint(x, pltpu.HBM)
                for x in (
                    source.reshape(FRAMES, W, C),
                    frame_counts,
                    tap_frames.T,
                    tap_weights.T,
                    kernel_one,
                    bias_one.reshape(1, C),
                    kernel_two,
                    bias_two.reshape(1, C),
                    upstream.reshape(CAP, W, C),
                )
            )
        )
        decoded, source_grad = pl.pallas_call(
            finish,
            out_shape=(
                jax.ShapeDtypeStruct((CAP, W, C), BF16),
                jax.ShapeDtypeStruct((FRAMES, W, C), F32),
            ),
            in_specs=[pl.BlockSpec(memory_space=pltpu.VMEM)] * 2,
            out_specs=[pl.BlockSpec(memory_space=pl.ANY)] * 2,
            scratch_shapes=[pltpu.SemaphoreType.DMA((2,))],
        )(*(pltpu.with_memory_space_constraint(x, pltpu.VMEM) for x in (decoded, source_grad)))
        return decoded.reshape(CAP, 1, W, C), source_grad.reshape(FRAMES, 1, W, C)

    whole = P("tm", "rows", None, None)
    return jax.shard_map(
        body,
        mesh=mesh,
        in_specs=(whole, P("tm"), P("tm", None), P("tm", None), P(), P(), P(), P(), whole),
        out_specs=(whole, whole),
        check_vma=False,
    )
```
